32 devices in a mesh: cam: 8 (over y, x, core), pts: 4 (over z).
Axes of the slice: x: 2, y: 2, z: 4, core: 2. Of those that a mesh axis runs over, the one named last changes fastest.
Arguments:
- rhs: float32 [9, 65536], P(None, 'cam'), may hold values from -6 to 6
- cam_block: float32 [9, 9, 65536], P(None, None, 'cam'), as said below
- coupling: bfloat16 [256, 144, 6144], P('pts', None, 'cam'), may hold values from -0.0390625 to 0.0390625
- point_inverse: float32 [3, 3, 16384], P(None, None, 'pts'), as said below
- precond: float32 [9, 9, 65536], P(None, None, 'cam'), as said below
- tile_index: int32 [256, 32], P('pts', 'cam'), may hold values from 0 to 511
- tile_count: int32 [256, 8], P('pts', 'cam'), may hold values from 1 to 4, as said below
Outputs:
- solution: float32 [9, 65536], P(None, 'cam')
- residual: float32 [9, 65536], P(None, 'cam')
The draws below stay inside these ranges and needn't reach their ends.
Inputs may be any that keep to these rules, and one draw needn't show every extreme that they name: `tile_count`: every entry is at least 1 and at most 4; both ends occur. `cam_block`: symmetric with a dominant positive diagonal for each camera. `precond`: symmetric with a dominant positive diagonal for each camera. `point_inverse`: symmetric with a dominant positive diagonal for each point.
All inputs are finite; a program needn't handle non-finite values.
Results may differ from the reference program's by a relative error of at most 0.0024.
Values may be sent and summed in bfloat16 or wider, within the bound.
No kernel may reach another device: no remote copies, remote signals or barrier semaphores. Data moves between devices by JAX's collectives and lax.ppermute only.
A program may use at most 128 MiB of HBM per device.

```python
import jax
import jax.numpy as jnp
from jax import lax

CAM_TILES = 512
PT_TILES = 64
SLOTS = 4
ITERS = 3
CAMS = 65536
POINT_TILES = 256
POINTS = 16384
SLOT_COLS = 32
N_CAM = 8
N_PTS = 4


def dominant_block(key, size, count, diag_lo, diag_hi, off_size):
    first, second = jax.random.split(key)
    diagonal = jax.random.uniform(first, (size, count), jnp.float32, diag_lo, diag_hi)
    offdiag = jax.random.uniform(second, (size, size, count), jnp.float32, -off_size, off_size)
    symmetric = (offdiag + offdiag.transpose(1, 0, 2)) * 0.5
    square_eye = jnp.arange(size)[:, None] == jnp.arange(size)[None, :]
    return jnp.where(square_eye[:, :, None], diagonal[:, None, :], symmetric)


def draw_cam_block(key, part):
    return dominant_block(key, 9, CAMS, 2.0, 4.0, 0.15)


def draw_precond(key, part):
    return dominant_block(key, 9, CAMS, 0.25, 0.5, 0.02)


def draw_point_inverse(key, part):
    return dominant_block(key, 3, POINTS, 0.5, 2.0, 0.2)


def draw_tile_count(key, part):
    counts = jax.random.randint(key, (POINT_TILES * N_CAM,), 1, SLOTS + 1, dtype=jnp.int32)
    counts = counts.at[0].set(SLOTS).at[1].set(1)
    return counts.reshape(POINT_TILES, N_CAM)


def touch_ends(drawn, own_key, low, largest):
    longest = drawn.shape.index(max(drawn.shape))
    spots = []
    for shift in (0, 1):
        where = [jax.random.randint(jax.random.fold_in(own_key, axis), (), 0, length) for axis, length in enumerate(drawn.shape)]
        where[longest] = (where[longest] + shift) % drawn.shape[longest]
        spots.append(tuple(where))
    return drawn.at[spots[0]].set(low).at[spots[1]].set(largest)


def block_levels(own_key, extent, cuts, low, high):
    gain, own = 1.0, jax.random.fold_in(own_key, 6)
    for axis_at, blocks in cuts:
        steps = jnp.exp(jax.random.uniform(jax.random.fold_in(own, axis_at), (blocks,), jnp.float32, low / len(cuts), high / len(cuts)))
        gain = gain * jnp.repeat(steps, extent[axis_at] // blocks).reshape([-1 if axis == axis_at else 1 for axis in range(len(extent))])
    return gain


def gaussian(key, shape, scale, reach, cuts=(), kind=jnp.bfloat16):
    result = jax.random.normal(key, shape, jnp.float32) * scale
    if len(cuts) > 0:
        result = block_levels(key, shape, cuts, -0.22, 0.18) * result
    return jnp.clip(result, min=-reach, max=reach).astype(kind)


def setup_inputs(seed: int = 0) -> dict:
    arg_keys = jax.random.split(jax.random.key(seed), 8)
    rhs = gaussian(arg_keys[0], (9, CAMS), 1.0, 6.0, ((1, 8),), jnp.float32)
    cam_block = draw_cam_block(jax.random.fold_in(arg_keys[7], 71), 0)
    coupling = gaussian(arg_keys[2], (POINT_TILES, 144, SLOT_COLS * 192), (4 * (N_CAM * SLOTS * 144 + PT_TILES * SLOTS * N_PTS * 192 // CAM_TILES)) ** -0.5, 0.0390625, ((0, 4), (2, 8)))
    point_inverse = draw_point_inverse(jax.random.fold_in(arg_keys[7], 71), 0)
    precond = draw_precond(jax.random.fold_in(arg_keys[7], 71), 0)
    tile_index = touch_ends(jax.random.randint(arg_keys[5], (POINT_TILES, SLOT_COLS), 0, CAM_TILES), jax.random.fold_in(arg_keys[5], 1), 0, CAM_TILES - 1).astype(jnp.int32)
    tile_count = draw_tile_count(jax.random.fold_in(arg_keys[7], 71), 0)
    return {"rhs": rhs, "cam_block": cam_block, "coupling": coupling, "point_inverse": point_inverse, "precond": precond, "tile_index": tile_index, "tile_count": tile_count}


def to_tiles(vector, width):
    comps, count = vector.shape
    return vector.reshape(comps, count // width, width).transpose(1, 0, 2).reshape(count // width, comps * width)


def from_tiles(tiles, comps):
    count, cols = tiles.shape
    width = cols // comps
    return tiles.reshape(count, comps, width).transpose(1, 0, 2).reshape(comps, count * width)


def reference(rhs, cam_block, coupling, point_inverse, precond, tile_index, tile_count):
    slot_cols = tile_index.shape[1]
    slot_pos = jnp.arange(slot_cols, dtype=jnp.int32)
    slot_group = slot_pos // SLOTS
    within = slot_pos % SLOTS
    global_tile = slot_group[None, :] * CAM_TILES + tile_index
    usable = (within[None, :] < tile_count[:, slot_group]).astype(jnp.float32)
    grouped = coupling.reshape(N_PTS, PT_TILES, 144, slot_cols, 192)

    def forward_block(pair):
        block, dir_rows = pair
        return jnp.einsum("sckp,skc->sp", block.astype(jnp.float32), dir_rows.astype(jnp.float32), precision=lax.Precision.HIGHEST)

    def backward_block(pair):
        block, solved_rows = pair
        return jnp.einsum("sckp,sp->skc", block.astype(jnp.float32), solved_rows.astype(jnp.float32), precision=lax.Precision.HIGHEST)

    def schur_apply(direction):
        dir_half = direction.astype(jnp.bfloat16)
        dir_tiles = to_tiles(dir_half, 16)
        dir_rows = dir_tiles[global_tile] * usable[:, :, None].astype(jnp.bfloat16)
        point_sum = lax.map(forward_block, (grouped, dir_rows.reshape(N_PTS, PT_TILES, slot_cols, 144)))
        point_sum = from_tiles(point_sum.reshape(N_PTS * PT_TILES, 192), 3)
        solved = jnp.sum(point_inverse * point_sum[None, :, :], axis=1).astype(jnp.bfloat16)
        solved_tiles = to_tiles(solved, 64).reshape(N_PTS, PT_TILES, 192)
        contrib = lax.map(backward_block, (grouped, solved_tiles))
        contrib = contrib.reshape(-1, 144) * usable.reshape(-1, 1)
        cam_tiles = jax.ops.segment_sum(contrib, global_tile.reshape(-1), num_segments=CAM_TILES * N_CAM)
        cam_term = from_tiles(cam_tiles, 9)
        return jnp.sum(cam_block * direction[None, :, :], axis=1) - cam_term

    solution = jnp.zeros_like(rhs)
    residual = rhs
    precond_res = jnp.sum(precond * residual[None, :, :], axis=1)
    direction = precond_res
    inner_now = jnp.sum(residual * precond_res)
    for iteration in range(ITERS):
        image = schur_apply(direction)
        step_size = inner_now / jnp.sum(direction * image)
        solution = solution + step_size * direction
        residual = residual - step_size * image
        if iteration + 1 < ITERS:
            precond_res = jnp.sum(precond * residual[None, :, :], axis=1)
            inner_new = jnp.sum(residual * precond_res)
            direction = precond_res + (inner_new / inner_now) * direction
            inner_now = inner_new
    return solution, residual
```

```python
import functools

import jax
import jax.numpy as jnp
from jax import lax
from jax.experimental import pallas as pl
from jax.experimental.pallas import tpu as pltpu
from jax.sharding import PartitionSpec as P


ITERS = 3
F32 = jnp.float32
BF16 = jnp.bfloat16
VMEM = pl.BlockSpec(memory_space=pltpu.VMEM)
HBM = pl.BlockSpec(memory_space=pltpu.HBM)
NT = (((1,), (1,)), ((), ()))
FETCHES = 8


def iota(shape, dim):
    return lax.broadcasted_iota(jnp.int32, shape, dim)


def tree_sum(values):
    while len(values) > 1:
        values = [a + b for a, b in zip(values[::2], values[1::2])] + values[
            len(values) - len(values) % 2 :
        ]
    return values[0]


def sym(size, i, j):
    i, j = min(i, j), max(i, j)
    return i * size - i * (i - 1) // 2 + (j - i)


def total(value):
    return jnp.sum(value, keepdims=True)


def pieces(value):
    high = value.astype(BF16).astype(F32)
    rest = value - high
    middle = rest.astype(BF16).astype(F32)
    return [high, middle, rest - middle]


def scalar_lanes(scalars, rows):
    lane = iota((rows, 64), 1)
    tile = jnp.zeros((rows, 64), F32)
    for at, piece in enumerate(p for s in scalars for p in pieces(s)):
        tile = jnp.where(lane == at, piece, tile)
    return tile


def read_scalars(tile, count):
    row = tile[0:1, :]
    return [
        row[:, 3 * n : 3 * n + 1] + row[:, 3 * n + 1 : 3 * n + 2] + row[:, 3 * n + 2 : 3 * n + 3]
        for n in range(count)
    ]


def sym_rows(matrix, size, rows, vector):
    return [
        tree_sum([matrix[sym(size, i, j), rows, :] * vector[j] for j in range(size)])
        for i in range(size)
    ]


def tile_onehot(row_a, row_q, tiles, planes):
    column = jnp.where(row_a >= 0, row_q * planes + row_a, -1.0).astype(jnp.int32)
    return jnp.where(iota((tiles, column.shape[1]), 0) == column, 1.0, 0.0).astype(BF16)


def to_tiles(z_ref, zt_ref):
    planes = z_ref.shape[1]
    for j in range(z_ref.shape[0]):
        turned = z_ref[j].T
        parts = [turned[16 * q : 16 * q + 16, :] for q in range(8)]
        zt_ref[16 * j : 16 * j + 16, :] = jnp.concatenate(parts, axis=1).astype(BF16)


def from_tiles(tiles, t4_ref):
    planes = t4_ref.shape[1]
    for j in range(t4_ref.shape[0]):
        block = tiles[16 * j : 16 * j + 16, :]
        parts = [block[:, q * planes : (q + 1) * planes] for q in range(8)]
        t4_ref[j] = jnp.concatenate(parts, axis=0).T


def gather_rows(zt_ref, onehot, rows_ref):
    rows_ref[...] = jnp.dot(zt_ref[...], onehot, preferred_element_type=F32).T


def forward_pairs(e_ref, rows_ref, part_ref, first, count, unroll):
    sub = iota((8, rows_ref.shape[1]), 0)

    def body(pair, carry):
        rows = rows_ref[pl.ds(pl.multiple_of(pair * 8, 8), 8), :]
        top = jnp.where(sub < 4, rows, 0.0).astype(BF16)
        low = jnp.where(sub >= 4, rows, 0.0).astype(BF16)
        part = jnp.dot(top, e_ref[2 * pair], preferred_element_type=F32) + jnp.dot(
            low, e_ref[2 * pair + 1], preferred_element_type=F32
        )
        for i in range(6):
            part_ref[i, pl.ds(pl.multiple_of(pair * 8, 8), 8), :] = part[:, 128 * i : 128 * i + 128]
        return carry

    lax.fori_loop(first, first + count, body, 0, unroll=unroll)


def forward_sum(part_ref, count):
    def pick(i, s):
        return part_ref[i, pl.ds(s, count, 4), :]

    even = jnp.concatenate([pick(0, 0) + pick(3, 2), pick(1, 0) + pick(4, 2)], axis=1)
    odd = jnp.concatenate([pick(1, 1) + pick(4, 3), pick(2, 1) + pick(5, 3)], axis=1)
    return even[:, :192] + odd[:, 64:]


def backward(e_ref, y, yc_ref, c_ref, unroll):
    count = e_ref.shape[0]
    wide = [jnp.concatenate(pair, axis=1) for pair in ((y[0], y[1]), (y[2], y[0]), (y[1], y[2]))]
    for i in range(6):
        yc_ref[:, 128 * i : 128 * i + 128] = wide[i % 3]
    row, col = iota((8, 768), 0), iota((8, 768), 1)
    masks = [(col >= 192 * (row - r)) & (col < 192 * (row - r) + 192) for r in (0, 4)]

    def body(pair, carry):
        part = None
        for k in range(2):
            wide_row = jnp.broadcast_to(yc_ref[pl.ds(2 * pair + k, 1), :], (8, 768))
            lhs = jnp.where(masks[k], wide_row, 0.0).astype(BF16)
            one = lax.dot_general(lhs, e_ref[2 * pair + k], NT, preferred_element_type=F32)
            part = one if part is None else part + one
        c_ref[pl.ds(pl.multiple_of(pair * 8, 8), 8), :] = part
        return carry

    lax.fori_loop(0, count // 2, body, 0, unroll=unroll)


def start_kernel(
    rhs_hbm, m_hbm, c_hbm, e_hbm, v_hbm, index_ref, count_ref,
    e_ref, m_ref, c_ref, v_ref, r_ref, z_ref, cz_ref, slot_ref, msg_ref,
    rn, mn, m8, cn, c8, vn, split, vrow, zt_ref, rows_ref, part_ref, sems, e_sems,
):
    planes, count = r_ref.shape[1], e_ref.shape[0]
    step = count // FETCHES
    inner = pl.ds(0, 8)
    copies = [
        pltpu.make_async_copy(src, dst, sems.at[n])
        for n, (src, dst) in enumerate(
            (
                (rhs_hbm, rn),
                (m_hbm.at[inner, inner], mn),
                (m_hbm.at[8], m8),
                (c_hbm.at[inner, inner], cn),
                (c_hbm.at[8], c8),
                (v_hbm, vn),
            )
        )
    ]
    for copy in copies:
        copy.start()

    def fetch(n):
        part = pl.ds(n * step, step)
        return pltpu.make_async_copy(e_hbm.at[part], e_ref.at[part], e_sems.at[n])

    for n in range(FETCHES):
        fetch(n).start()

    def split_rows(src, buffer):
        def body(a, carry):
            lanes = pl.ds(pl.multiple_of(a * 128, 128), 128)
            buffer[pl.ds(pl.multiple_of(a * 8, 8), 8), :] = src[inner, lanes]
            return carry

        lax.fori_loop(0, planes, body, 0, unroll=16)

    def split_last(src, store):
        def body(a, carry):
            lanes = pl.ds(pl.multiple_of(a * 128, 128), 128)
            store(a, src[pl.ds(8, 1), lanes])
            return carry

        lax.fori_loop(0, planes, body, 0, unroll=16)

    def split_matrix(inner_ref, last_ref, out_ref):
        for i in range(9):
            buffer = split.at[i % 2]
            split_rows(inner_ref.at[i] if i < 8 else last_ref, buffer)
            for j in range(i if i < 8 else 0, 8):
                out_ref[sym(9, i, j)] = buffer[pl.ds(j, planes, 8), :]

        def store(a, row):
            out_ref[sym(9, 8, 8), pl.ds(a, 1), :] = row

        split_last(last_ref, store)

    slots = index_ref.shape[1]
    index = index_ref[...]
    used = iota(index.shape, 1) < count_ref[...]
    spread = jnp.where(iota((count, count * slots), 1) // slots == iota((count, count * slots), 0), 1.0, 0.0)
    mine = iota((8, count * slots), 1) % slots == iota((8, count * slots), 0)
    pad = jnp.zeros((count, 128 - slots), F32)
    slot_rows = []
    for part in (jnp.where(used, index // 8, -1), index % 8):
        turned = jnp.concatenate([part.astype(F32), pad], axis=1).T[0:8, :]
        moved = jnp.dot(turned.astype(BF16), spread.astype(BF16), preferred_element_type=F32)
        slot_rows.append(jnp.sum(jnp.where(mine, moved, 0.0), axis=0, keepdims=True))
    row = iota((8, count * slots), 0)
    slot_ref[...] = jnp.where(row == 0, slot_rows[0], jnp.where(row == 1, slot_rows[1], 0.0))
    onehot = tile_onehot(slot_rows[0], slot_rows[1], 8 * planes, planes)

    copies[0].wait()
    split_rows(rn, split.at[0])
    for j in range(8):
        r_ref[j] = split[0, pl.ds(j, planes, 8), :]

    def store_last(a, value):
        r_ref[8, pl.ds(a, 1), :] = value

    split_last(rn, store_last)
    copies[1].wait()
    copies[2].wait()
    split_matrix(mn, m8, m_ref)

    def precondition(g, inner_sum):
        rows = pl.ds(pl.multiple_of(g * 8, 8), 8)
        r = [r_ref[j, rows, :] for j in range(9)]
        z = sym_rows(m_ref, 9, rows, r)
        for j in range(9):
            z_ref[j, rows, :] = z[j]
        return inner_sum + tree_sum([a * b for a, b in zip(r, z)])

    zero = jnp.zeros((8, 128), F32)
    inner_sum = lax.fori_loop(0, planes // 8, precondition, zero)
    to_tiles(z_ref, zt_ref)
    gather_rows(zt_ref, onehot, rows_ref)

    copies[3].wait()
    copies[4].wait()
    split_matrix(cn, c8, c_ref)

    def apply_camera(g, curve):
        rows = pl.ds(pl.multiple_of(g * 8, 8), 8)
        z = [z_ref[j, rows, :] for j in range(9)]
        cz = sym_rows(c_ref, 9, rows, z)
        for j in range(9):
            cz_ref[j, rows, :] = cz[j]
        return curve + tree_sum([a * b for a, b in zip(z, cz)])

    curve = lax.fori_loop(0, planes // 8, apply_camera, zero)

    copies[5].wait()
    half = vrow.shape[0]
    for i in range(3):
        for j in range(i, 3):

            def body(u, carry):
                lanes = pl.ds(pl.multiple_of(u * 128, 128), 128)
                vrow[pl.ds(u, 1), :] = vn[i, j : j + 1, lanes]
                return carry

            lax.fori_loop(0, half, body, 0, unroll=16)
            plane = vrow[...]
            v_ref[sym(3, i, j), pl.ds(0, half, 2), :] = plane
            v_ref[sym(3, i, j), pl.ds(1, half, 2), :] = jnp.concatenate(
                [plane[:, 64:], plane[:, :64]], axis=1
            )

    def chunk(n, carry):
        fetch(n).wait()
        forward_pairs(e_ref, rows_ref, part_ref, n * (step // 2), step // 2, True)
        return carry

    lax.fori_loop(0, FETCHES, chunk, 0)
    scalars = scalar_lanes([total(inner_sum), total(curve), jnp.zeros((1, 1), F32)], count)
    msg_ref[...] = jnp.concatenate([forward_sum(part_ref, count), scalars], axis=1).astype(BF16)


def pair_kernel(*refs):
    *in_refs, out_ref = refs
    value = tree_sum([ref[...].astype(F32) for ref in in_refs])
    scalars = scalar_lanes(read_scalars(value[:, 192:], 3), value.shape[0])
    out_ref[...] = jnp.concatenate([value[:, :192], scalars], axis=1).astype(BF16)


def points_kernel(parts, first, *refs):
    summed = tree_sum([ref[...].astype(F32) for ref in refs[:parts]])
    refs = refs[parts:]
    if not first:
        p_old_ref, scal_old_ref, *refs = refs
    e_ref, v_ref, slot_ref, msg_ref, p_ref, scal_ref, yc_ref, c_ref = refs
    inner_now, z_c_z, z_c_d = read_scalars(summed[:, 192:], 3)
    point_sum = summed[:, :192]
    beta, curve = jnp.zeros((1, 1), F32), z_c_z
    if not first:
        beta = inner_now / scal_old_ref[0:1, 0:1]
        curve = z_c_z + beta * (2.0 * z_c_d + beta * scal_old_ref[1:2, 0:1])
        point_sum = point_sum + beta * p_old_ref[...]
    p_ref[...] = point_sum
    row = iota((8, 128), 0)
    scal_ref[...] = jnp.where(row == 0, inner_now, jnp.where(row == 1, curve, beta))
    p = [point_sum[:, 64 * i : 64 * i + 64] for i in range(3)]
    y = [tree_sum([v_ref[sym(3, i, j)][:, :64] * p[j] for j in range(3)]) for i in range(3)]
    taken = total(tree_sum([a * b for a, b in zip(p, y)]))
    backward(e_ref, y, yc_ref, c_ref, 16)
    rows = c_ref.shape[1]
    msg_ref[0:rows, :] = c_ref[...].T.astype(BF16)
    width = msg_ref.shape[1]
    row = iota((16, width), 0)
    tail = jnp.zeros((16, width), F32)
    for at, value in enumerate([slot_ref[0:1, :], slot_ref[1:2, :], *pieces(taken)]):
        tail = jnp.where(row == at, value, tail)
    msg_ref[rows : rows + 16, :] = tail.astype(BF16)


def camera_kernel(parts, first, last, *refs):
    msgs, refs = refs[:parts], refs[parts:]
    scal_ref, z_ref, cz_ref, r_ref, *refs = refs
    if not first:
        d_old_ref, cd_old_ref, sol_old_ref, *refs = refs
    if last:
        sol_out, res_out, all_ref, t4_ref, sol_ref, split = refs
        res_ref = t4_ref
    else:
        e_ref, m_ref, c_ref, slot_ref, *refs = refs
        msg_ref, res_ref, sol_ref, zn_ref, czn_ref, *refs = refs
        if not first:
            d_ref, cd_ref, *refs = refs
        all_ref, t4_ref, zt_ref, rows_ref, part_ref = refs
    planes = z_ref.shape[1]
    rows_all = all_ref.shape[1] - 16
    me = lax.axis_index("pts")
    for k in range(parts):
        all_ref[me ^ k] = msgs[k][...]
    taken, tiles = [], []
    for k in range(parts):
        tail = all_ref[k, rows_all : rows_all + 16, :].astype(F32)
        taken.append(tail[2:3, 0:1] + tail[3:4, 0:1] + tail[4:5, 0:1])
        onehot = tile_onehot(tail[0:1, :], tail[1:2, :], 8 * planes, planes)
        tiles.append(
            lax.dot_general(all_ref[k, 0:rows_all, :], onehot, NT, preferred_element_type=F32)
        )
    inner_now, curve, beta = scal_ref[0:1, 0:1], scal_ref[1:2, 0:1], scal_ref[2:3, 0:1]
    step_size = inner_now / (curve - tree_sum(taken))
    from_tiles(tree_sum(tiles), t4_ref)

    def update(g, sums):
        rows = pl.ds(pl.multiple_of(g * 8, 8), 8)
        r, cd = [], []
        for j in range(9):
            d, c_d = z_ref[j, rows, :], cz_ref[j, rows, :]
            if not first:
                d = d + beta * d_old_ref[j, rows, :]
                c_d = c_d + beta * cd_old_ref[j, rows, :]
                if not last:
                    d_ref[j, rows, :] = d
                    cd_ref[j, rows, :] = c_d
            step = step_size * d
            sol_ref[j, rows, :] = step if first else sol_old_ref[j, rows, :] + step
            r.append(r_ref[j, rows, :] - step_size * (c_d - t4_ref[j, rows, :]))
            cd.append(c_d)
        for j in range(9):
            res_ref[j, rows, :] = r[j]
        if last:
            return sums
        z = sym_rows(m_ref, 9, rows, r)
        cz = sym_rows(c_ref, 9, rows, z)
        for j in range(9):
            zn_ref[j, rows, :] = z[j]
            czn_ref[j, rows, :] = cz[j]
        pairs = (zip(r, z), zip(z, cz), zip(z, cd))
        return tuple(s + tree_sum([a * b for a, b in p]) for s, p in zip(sums, pairs))

    sums = lax.fori_loop(0, planes // 8, update, (jnp.zeros((8, 128), F32),) * 3)
    if last:
        for src, dst in ((sol_ref, sol_out), (res_ref, res_out)):
            for j in range(8):
                split[pl.ds(j, planes, 8), :] = src[j]

            def body(a, carry):
                lanes = pl.ds(pl.multiple_of(a * 128, 128), 128)
                dst[0:8, lanes] = split[pl.ds(pl.multiple_of(a * 8, 8), 8), :]
                dst[8:9, lanes] = src[8, pl.ds(a, 1), :]
                return carry

            lax.fori_loop(0, planes, body, 0, unroll=16)
        return
    to_tiles(zn_ref, zt_ref)
    onehot = tile_onehot(slot_ref[0:1, :], slot_ref[1:2, :], 8 * planes, planes)
    gather_rows(zt_ref, onehot, rows_ref)
    count = e_ref.shape[0]
    forward_pairs(e_ref, rows_ref, part_ref, 0, count // 2, 16)
    scalars = scalar_lanes([total(s) for s in sums], count)
    msg_ref[...] = jnp.concatenate([forward_sum(part_ref, count), scalars], axis=1).astype(BF16)


def per_device(n_cam, n_pts, rhs, cam_block, coupling, point_inverse, precond, tile_index, tile_count):
    count, slots = tile_index.shape
    size, cams = rhs.shape
    rows, cols = coupling.shape[1:]
    planes, tiles, width = cams // 128, cams // 16, count * slots
    points = point_inverse.shape[2]
    shape = jax.ShapeDtypeStruct
    vector = shape((size, planes, 128), F32)
    message = shape((count, 256), BF16)
    planes_of = size * (size + 1) // 2
    part_scratch = pltpu.VMEM((cols // 128, width, 128), F32)
    rows_scratch = pltpu.VMEM((width, rows), F32)
    zt_scratch = pltpu.VMEM((rows, tiles), BF16)

    def call(kernel, outs, args, in_specs=None, scratch=(), megabytes=8, name=None):
        return pl.pallas_call(
            kernel,
            out_shape=outs,
            in_specs=in_specs or [VMEM] * len(args),
            out_specs=jax.tree.map(lambda _: VMEM, outs),
            scratch_shapes=list(scratch),
            compiler_params=pltpu.CompilerParams(vmem_limit_bytes=megabytes * 2**20),
            name=name,
        )(*args)

    def exchange(value, axis, axis_size, masks):
        return [value] + [
            lax.ppermute(value, axis, [(i, i ^ k) for i in range(axis_size)]) for k in masks
        ]

    coupling, m4, c4, v6, residual, z, cz, slot, message_now = call(
        start_kernel,
        [
            pltpu.VMEM(coupling.shape, BF16),
            pltpu.VMEM((planes_of, planes, 128), F32),
            pltpu.VMEM((planes_of, planes, 128), F32),
            pltpu.VMEM((6, count, 128), F32),
            vector,
            vector,
            vector,
            shape((8, width), F32),
            message,
        ],
        (rhs, precond, cam_block, coupling, point_inverse, tile_index, tile_count),
        in_specs=[HBM] * 5 + [VMEM] * 2,
        scratch=[
            pltpu.VMEM((size, cams), F32),
            pltpu.VMEM((8, 8, cams), F32),
            pltpu.VMEM((size, cams), F32),
            pltpu.VMEM((8, 8, cams), F32),
            pltpu.VMEM((size, cams), F32),
            pltpu.VMEM((3, 3, points), F32),
            pltpu.VMEM((2, 8 * planes, 128), F32),
            pltpu.VMEM((points // 128, 128), F32),
            zt_scratch,
            rows_scratch,
            part_scratch,
            pltpu.SemaphoreType.DMA((6,)),
            pltpu.SemaphoreType.DMA((FETCHES,)),
        ],
        megabytes=16,
        name="start",
    )
    inner = max(1, n_cam // 4)
    old_points, old_camera = (), ()
    for iteration in range(ITERS):
        first, last = iteration == 0, iteration + 1 == ITERS
        if inner > 1:
            pair = exchange(message_now, "cam", n_cam, range(1, inner))
            message_now = call(pair_kernel, message, pair, name="pair")
        parts = exchange(message_now, "cam", n_cam, range(inner, n_cam, inner))
        tile_message, point_sum, scal = call(
            functools.partial(points_kernel, len(parts), first),
            [
                shape((rows + 16, width), BF16),
                shape((count, 192), F32),
                shape((8, 128), F32),
            ],
            (*parts, *old_points, coupling, v6, slot),
            scratch=[pltpu.VMEM((count, cols), F32), rows_scratch],
            name="points",
        )
        old_points = (point_sum, scal)
        parts = exchange(tile_message, "pts", n_pts, range(1, n_pts))
        kernel = functools.partial(camera_kernel, len(parts), first, last)
        common = [
            pltpu.VMEM((n_pts, rows + 16, width), BF16),
            pltpu.VMEM((size, planes, 128), F32),
        ]
        args = (*parts, scal, z, cz, residual, *old_camera)
        if last:
            plain = shape((size, cams), F32)
            scratch = [*common, pltpu.VMEM((size, planes, 128), F32), pltpu.VMEM((8 * planes, 128), F32)]
            return tuple(call(kernel, [plain, plain], args, scratch=scratch, name="finish"))
        outs = [message, vector, vector, vector, vector] + ([] if first else [vector, vector])
        message_now, residual, solution, z_new, cz_new, *direction = call(
            kernel,
            outs,
            (*args, coupling, m4, c4, slot),
            scratch=[*common, zt_scratch, rows_scratch, part_scratch],
            name="camera",
        )
        d, cd = direction if direction else (z, cz)
        old_camera = (d, cd, solution)
        z, cz = z_new, cz_new


def solution(mesh):
    in_specs = (
        P(None, "cam"),
        P(None, None, "cam"),
        P("pts", None, "cam"),
        P(None, None, "pts"),
        P(None, None, "cam"),
        P("pts", "cam"),
        P("pts", "cam"),
    )
    out_specs = (P(None, "cam"), P(None, "cam"))
    return jax.shard_map(
        functools.partial(per_device, mesh.shape["cam"], mesh.shape["pts"]),
        mesh=mesh,
        in_specs=in_specs,
        out_specs=out_specs,
        check_vma=False,
    )
```

```python
import functools

import jax
import jax.numpy as jnp
from jax import lax
from jax.experimental import pallas as pl
from jax.experimental.pallas import tpu as pltpu
from jax.sharding import PartitionSpec as P


ITERS = 3
F32 = jnp.float32
BF16 = jnp.bfloat16
VMEM = pl.BlockSpec(memory_space=pltpu.VMEM)
HBM = pl.BlockSpec(memory_space=pltpu.HBM)
NT = (((1,), (1,)), ((), ()))
FETCHES = 8
TAIL = 8


def in_hbm(value):
    return pltpu.with_memory_space_constraint(value, pltpu.HBM)


def iota(shape, dim):
    return lax.broadcasted_iota(jnp.int32, shape, dim)


def tree_sum(values):
    while len(values) > 1:
        values = [a + b for a, b in zip(values[::2], values[1::2])] + values[
            len(values) - len(values) % 2 :
        ]
    return values[0]


def sym(size, i, j):
    i, j = min(i, j), max(i, j)
    return i * size - i * (i - 1) // 2 + (j - i)


def total(value):
    return jnp.sum(value, keepdims=True)


def pieces(value):
    high = value.astype(BF16).astype(F32)
    rest = value - high
    middle = rest.astype(BF16).astype(F32)
    return [high, middle, rest - middle]


def scalar_lanes(scalars, rows):
    lane = iota((rows, 64), 1)
    tile = jnp.zeros((rows, 64), F32)
    for at, piece in enumerate(p for s in scalars for p in pieces(s)):
        tile = jnp.where(lane == at, piece, tile)
    return tile


def read_scalars(tile, count):
    row = tile[0:1, :]
    return [
        row[:, 3 * n : 3 * n + 1] + row[:, 3 * n + 1 : 3 * n + 2] + row[:, 3 * n + 2 : 3 * n + 3]
        for n in range(count)
    ]


def sym_rows(matrix, size, rows, vector):
    return [
        tree_sum([matrix[sym(size, i, j), rows, :] * vector[j] for j in range(size)])
        for i in range(size)
    ]


def tile_onehot(rows, tiles, planes):
    row_a, row_q = rows[0:1, :], rows[1:2, :]
    at = jnp.where(row_a >= 0, row_q * planes + row_a, -1.0).astype(jnp.int32)
    return jnp.where(iota((tiles, at.shape[1]), 0) == at, 1.0, 0.0).astype(BF16)


def to_tiles(z_ref, zt_ref):
    planes = z_ref.shape[1]
    for j in range(z_ref.shape[0]):
        turned = z_ref[j].T
        parts = [turned[16 * q : 16 * q + 16, :] for q in range(8)]
        zt_ref[16 * j : 16 * j + 16, :] = jnp.concatenate(parts, axis=1).astype(BF16)


def from_tiles(tiles, t4_ref):
    planes = t4_ref.shape[1]
    for j in range(t4_ref.shape[0]):
        block = tiles[16 * j : 16 * j + 16, :]
        parts = [block[:, q * planes : (q + 1) * planes] for q in range(8)]
        t4_ref[j] = jnp.concatenate(parts, axis=0).T


def gather_rows(zt_ref, onehot, rows_ref):
    rows_ref[...] = jnp.dot(zt_ref[...], onehot, preferred_element_type=F32).T


def forward_pairs(e_ref, rows_ref, part_ref, pairs):
    sub = iota((8, rows_ref.shape[1]), 0)
    for pair in pairs:
        at = pl.ds(8 * pair, 8)
        rows = rows_ref[at, :]
        top = jnp.where(sub < 4, rows, 0.0).astype(BF16)
        low = jnp.where(sub >= 4, rows, 0.0).astype(BF16)
        part = jnp.dot(top, e_ref[2 * pair], preferred_element_type=F32) + jnp.dot(
            low, e_ref[2 * pair + 1], preferred_element_type=F32
        )
        for i in range(part_ref.shape[0]):
            part_ref[i, at, :] = part[:, 128 * i : 128 * i + 128]


def forward_sum(part_ref, count):
    def pick(i, s):
        return part_ref[i, pl.ds(s, count, 4), :]

    even = jnp.concatenate([pick(0, 0) + pick(3, 2), pick(1, 0) + pick(4, 2)], axis=1)
    odd = jnp.concatenate([pick(1, 1) + pick(4, 3), pick(2, 1) + pick(5, 3)], axis=1)
    return even[:, :192] + odd[:, 64:]


def backward(e_ref, y, yc_ref, c_ref):
    count = e_ref.shape[0]
    wide = [jnp.concatenate(pair, axis=1) for pair in ((y[0], y[1]), (y[2], y[0]), (y[1], y[2]))]
    for i in range(6):
        yc_ref[:, 128 * i : 128 * i + 128] = wide[i % 3]
    row, col = iota((8, 768), 0), iota((8, 768), 1)
    masks = [(col >= 192 * (row - r)) & (col < 192 * (row - r) + 192) for r in (0, 4)]

    for pair in range(count // 2):
        part = None
        for k in range(2):
            wide_row = jnp.broadcast_to(yc_ref[pl.ds(2 * pair + k, 1), :], (8, 768))
            lhs = jnp.where(masks[k], wide_row, 0.0).astype(BF16)
            one = lax.dot_general(lhs, e_ref[2 * pair + k], NT, preferred_element_type=F32)
            part = one if part is None else part + one
        c_ref[pl.ds(8 * pair, 8), :] = part


def start_kernel(
    rhs_hbm, m_hbm, c_hbm, e_hbm, v_hbm, index_hbm, count_hbm,
    e_ref, m_ref, c_ref, v_ref, r_ref, z_ref, cz_ref, slot_ref, msg_ref,
    rn, mn, m8, cn, c8, vn, index_ref, count_ref, split, vrow, zt_ref, rows_ref, part_ref, sems, e_sems,
):
    planes, count = r_ref.shape[1], e_ref.shape[0]
    step = count // FETCHES
    inner = pl.ds(0, 8)

    def fetch(n):
        part = pl.ds(n * step, step)
        return pltpu.make_async_copy(e_hbm.at[part], e_ref.at[part], e_sems.at[n])

    def copy(n, src, dst):
        return pltpu.make_async_copy(src, dst, sems.at[n])

    indices = [copy(0, index_hbm, index_ref), copy(1, count_hbm, count_ref)]
    rhs = [copy(2, rhs_hbm, rn)]
    precond = [copy(3, m_hbm.at[inner, inner], mn), copy(4, m_hbm.at[8], m8)]
    camera = [copy(5, c_hbm.at[inner, inner], cn), copy(6, c_hbm.at[8], c8)]
    inverse = [copy(7, v_hbm, vn)]
    early = [fetch(n) for n in range(FETCHES // 2)]
    late = [fetch(n) for n in range(FETCHES // 2, FETCHES)]
    for one in rhs + precond + indices + early + camera + inverse + late:
        one.start()

    def wait(copies):
        for one in copies:
            one.wait()

    def split_rows(src, buffer, used):
        for a in range(src.shape[1] // 128):
            buffer[8 * a : 8 * a + used, :] = src[0:used, 128 * a : 128 * a + 128]

    def split_last(src, out_ref, at):
        for a in range(planes):
            out_ref[at, a : a + 1, :] = src[8:9, 128 * a : 128 * a + 128]

    def split_matrix(inner_ref, last_ref, out_ref):
        for i in range(9):
            buffer = split.at[i % 2]
            split_rows(inner_ref.at[i] if i < 8 else last_ref, buffer, 8)
            for j in range(i if i < 8 else 0, 8):
                out_ref[sym(9, i, j)] = buffer[pl.ds(j, planes, 8), :]
        split_last(last_ref, out_ref, sym(9, 8, 8))

    wait(rhs)
    split_rows(rn, split.at[0], 8)
    for j in range(8):
        r_ref[j] = split[0, pl.ds(j, planes, 8), :]
    split_last(rn, r_ref, 8)

    wait(indices)
    slots = index_ref.shape[0]
    width = count * slots
    index = index_ref[...]
    used = iota(index.shape, 0) < count_ref[...]
    spread = jnp.where(iota((count, width), 1) // slots == iota((count, width), 0), 1.0, 0.0)
    mine = iota((8, width), 1) % slots == iota((8, width), 0)
    pad = jnp.zeros((8 - slots, count), F32)
    slot_rows = []
    for part in (jnp.where(used, index // 8, -1), index % 8):
        padded = jnp.concatenate([part.astype(F32), pad], axis=0).astype(BF16)
        moved = jnp.dot(padded, spread.astype(BF16), preferred_element_type=F32)
        slot_rows.append(jnp.sum(jnp.where(mine, moved, 0.0), axis=0, keepdims=True))
    row = iota((8, width), 0)
    slot_ref[...] = jnp.where(row == 0, slot_rows[0], jnp.where(row == 1, slot_rows[1], 0.0))
    onehot = tile_onehot(slot_ref[...], 8 * planes, planes)

    wait(precond)
    split_matrix(mn, m8, m_ref)

    def precondition(g, inner_sum):
        rows = pl.ds(pl.multiple_of(g * 8, 8), 8)
        r = [r_ref[j, rows, :] for j in range(9)]
        z = sym_rows(m_ref, 9, rows, r)
        for j in range(9):
            z_ref[j, rows, :] = z[j]
        return inner_sum + tree_sum([a * b for a, b in zip(r, z)])

    zero = jnp.zeros((8, 128), F32)
    inner_sum = lax.fori_loop(0, planes // 8, precondition, zero, unroll=True)
    to_tiles(z_ref, zt_ref)
    gather_rows(zt_ref, onehot, rows_ref)

    def forward_chunk(n, one):
        one.wait()
        forward_pairs(e_ref, rows_ref, part_ref, range(n * (step // 2), (n + 1) * (step // 2)))

    for n, one in enumerate(early):
        forward_chunk(n, one)

    wait(camera)
    split_matrix(cn, c8, c_ref)

    def apply_camera(g, curve):
        rows = pl.ds(pl.multiple_of(g * 8, 8), 8)
        z = [z_ref[j, rows, :] for j in range(9)]
        cz = sym_rows(c_ref, 9, rows, z)
        for j in range(9):
            cz_ref[j, rows, :] = cz[j]
        return curve + tree_sum([a * b for a, b in zip(z, cz)])

    curve = lax.fori_loop(0, planes // 8, apply_camera, zero, unroll=True)

    wait(inverse)
    half = vrow.shape[0]
    for i in range(3):
        split_rows(vn.at[i], split.at[i % 2], 3)
        for j in range(i, 3):
            plane = split[i % 2, pl.ds(j, half, 8), :]
            v_ref[sym(3, i, j), pl.ds(0, half, 2), :] = plane
            v_ref[sym(3, i, j), pl.ds(1, half, 2), :] = jnp.concatenate(
                [plane[:, 64:], plane[:, :64]], axis=1
            )

    for n, one in enumerate(late):
        forward_chunk(len(early) + n, one)
    scalars = scalar_lanes([total(inner_sum), total(curve), jnp.zeros((1, 1), F32)], count)
    msg_ref[...] = jnp.concatenate([forward_sum(part_ref, count), scalars], axis=1).astype(BF16)


def pair_kernel(*refs):
    *in_refs, out_ref = refs
    value = tree_sum([ref[...].astype(F32) for ref in in_refs])
    scalars = scalar_lanes(read_scalars(value[:, 192:], 3), value.shape[0])
    out_ref[...] = jnp.concatenate([value[:, :192], scalars], axis=1).astype(BF16)


def points_kernel(parts, first, *refs):
    summed = tree_sum([ref[...].astype(F32) for ref in refs[:parts]])
    refs = refs[parts:]
    if not first:
        p_old_ref, scal_old_ref, *refs = refs
    e_ref, v_ref, slot_ref, msg_ref, p_ref, scal_ref, yc_ref, c_ref = refs
    inner_now, z_c_z, z_c_d = read_scalars(summed[:, 192:], 3)
    point_sum = summed[:, :192]
    beta, curve = jnp.zeros((1, 1), F32), z_c_z
    if not first:
        beta = inner_now / scal_old_ref[0:1, 0:1]
        curve = z_c_z + beta * (2.0 * z_c_d + beta * scal_old_ref[1:2, 0:1])
        point_sum = point_sum + beta * p_old_ref[...]
    p_ref[...] = point_sum
    row = iota((8, 128), 0)
    scal_ref[...] = jnp.where(row == 0, inner_now, jnp.where(row == 1, curve, beta))
    p = [point_sum[:, 64 * i : 64 * i + 64] for i in range(3)]
    y = [tree_sum([v_ref[sym(3, i, j)][:, :64] * p[j] for j in range(3)]) for i in range(3)]
    taken = total(tree_sum([a * b for a, b in zip(p, y)]))
    backward(e_ref, y, yc_ref, c_ref)
    rows = c_ref.shape[1]
    msg_ref[0:rows, :] = c_ref[...].T.astype(BF16)
    width = msg_ref.shape[1]
    row = iota((TAIL, width), 0)
    tail = jnp.zeros((TAIL, width), F32)
    for at, value in enumerate([slot_ref[0:1, :], slot_ref[1:2, :], *pieces(taken)]):
        tail = jnp.where(row == at, value, tail)
    msg_ref[rows : rows + TAIL, :] = tail.astype(BF16)


def camera_kernel(parts, first, last, *refs):
    msgs, refs = refs[:parts], refs[parts:]
    scal_ref, z_ref, cz_ref, r_ref, *refs = refs
    if not first:
        d_old_ref, cd_old_ref, sol_old_ref, *refs = refs
    if last:
        sol_out, res_out, all_ref, t4_ref, sol_ref, split = refs
        res_ref = t4_ref
    else:
        e_ref, m_ref, c_ref, slot_ref, *refs = refs
        msg_ref, res_ref, sol_ref, zn_ref, czn_ref, *refs = refs
        if not first:
            d_ref, cd_ref, *refs = refs
        all_ref, t4_ref, zt_ref, rows_ref, part_ref = refs
    planes = z_ref.shape[1]
    rows_all = all_ref.shape[1] - TAIL
    me = lax.axis_index("pts")
    for k in range(parts):
        all_ref[me ^ k] = msgs[k][...]
    taken, tiles = [], []
    for k in range(parts):
        tail = all_ref[k, rows_all : rows_all + TAIL, :].astype(F32)
        taken.append(tail[2:3, 0:1] + tail[3:4, 0:1] + tail[4:5, 0:1])
        onehot = tile_onehot(tail, 8 * planes, planes)
        tiles.append(
            lax.dot_general(all_ref[k, 0:rows_all, :], onehot, NT, preferred_element_type=F32)
        )
    inner_now, curve, beta = scal_ref[0:1, 0:1], scal_ref[1:2, 0:1], scal_ref[2:3, 0:1]
    step_size = inner_now / (curve - tree_sum(taken))
    from_tiles(tree_sum(tiles), t4_ref)

    def update(g, sums):
        rows = pl.ds(pl.multiple_of(g * 8, 8), 8)
        r, cd = [], []
        for j in range(9):
            d, c_d = z_ref[j, rows, :], cz_ref[j, rows, :]
            if not first:
                d = d + beta * d_old_ref[j, rows, :]
                c_d = c_d + beta * cd_old_ref[j, rows, :]
                if not last:
                    d_ref[j, rows, :] = d
                    cd_ref[j, rows, :] = c_d
            step = step_size * d
            sol_ref[j, rows, :] = step if first else sol_old_ref[j, rows, :] + step
            r.append(r_ref[j, rows, :] - step_size * (c_d - t4_ref[j, rows, :]))
            cd.append(c_d)
        for j in range(9):
            res_ref[j, rows, :] = r[j]
        if last:
            return sums
        z = sym_rows(m_ref, 9, rows, r)
        cz = sym_rows(c_ref, 9, rows, z)
        for j in range(9):
            zn_ref[j, rows, :] = z[j]
            czn_ref[j, rows, :] = cz[j]
        pairs = (zip(r, z), zip(z, cz), zip(z, cd))
        return tuple(s + tree_sum([a * b for a, b in p]) for s, p in zip(sums, pairs))

    sums = lax.fori_loop(0, planes // 8, update, (jnp.zeros((8, 128), F32),) * 3, unroll=True)
    if last:
        for src, dst in ((sol_ref, sol_out), (res_ref, res_out)):
            for j in range(8):
                split[pl.ds(j, planes, 8), :] = src[j]

            def body(a, carry):
                lanes = pl.ds(pl.multiple_of(a * 128, 128), 128)
                dst[0:8, lanes] = split[pl.ds(pl.multiple_of(a * 8, 8), 8), :]
                dst[8:9, lanes] = src[8, pl.ds(a, 1), :]
                return carry

            lax.fori_loop(0, planes, body, 0, unroll=16)
        return
    to_tiles(zn_ref, zt_ref)
    onehot = tile_onehot(slot_ref[...], 8 * planes, planes)
    gather_rows(zt_ref, onehot, rows_ref)
    count = e_ref.shape[0]
    forward_pairs(e_ref, rows_ref, part_ref, range(count // 2))
    scalars = scalar_lanes([total(s) for s in sums], count)
    msg_ref[...] = jnp.concatenate([forward_sum(part_ref, count), scalars], axis=1).astype(BF16)


def per_device(n_cam, n_pts, rhs, cam_block, coupling, point_inverse, precond, tile_index, tile_count):
    count, slots = tile_index.shape
    size, cams = rhs.shape
    rows, cols = coupling.shape[1:]
    planes, tiles, width = cams // 128, cams // 16, count * slots
    points = point_inverse.shape[2]
    shape = jax.ShapeDtypeStruct
    vector = shape((size, planes, 128), F32)
    message = shape((count, 256), BF16)
    planes_of = size * (size + 1) // 2
    part_scratch = pltpu.VMEM((cols // 128, width, 128), F32)
    rows_scratch = pltpu.VMEM((width, rows), F32)
    zt_scratch = pltpu.VMEM((rows, tiles), BF16)

    def call(kernel, outs, args, in_specs=None, scratch=(), megabytes=8, name=None):
        return pl.pallas_call(
            kernel,
            out_shape=outs,
            in_specs=in_specs or [VMEM] * len(args),
            out_specs=jax.tree.map(lambda _: VMEM, outs),
            scratch_shapes=list(scratch),
            compiler_params=pltpu.CompilerParams(vmem_limit_bytes=megabytes * 2**20),
            name=name,
        )(*args)

    def exchange(value, axis, axis_size, masks):
        return [value] + [
            lax.ppermute(value, axis, [(i, i ^ k) for i in range(axis_size)]) for k in masks
        ]

    coupling, m4, c4, v6, residual, z, cz, slot, message_now = call(
        start_kernel,
        [
            pltpu.VMEM(coupling.shape, BF16),
            pltpu.VMEM((planes_of, planes, 128), F32),
            pltpu.VMEM((planes_of, planes, 128), F32),
            pltpu.VMEM((6, count, 128), F32),
            vector,
            vector,
            vector,
            shape((8, width), F32),
            message,
        ],
        [
            in_hbm(value)
            for value in (
                rhs, precond, cam_block, coupling, point_inverse, tile_index.T, tile_count.T,
            )
        ],
        in_specs=[HBM] * 7,
        scratch=[
            pltpu.VMEM((size, cams), F32),
            pltpu.VMEM((8, 8, cams), F32),
            pltpu.VMEM((size, cams), F32),
            pltpu.VMEM((8, 8, cams), F32),
            pltpu.VMEM((size, cams), F32),
            pltpu.VMEM((3, 3, points), F32),
            pltpu.VMEM((slots, count), jnp.int32),
            pltpu.VMEM((1, count), jnp.int32),
            pltpu.VMEM((2, 8 * planes, 128), F32),
            pltpu.VMEM((points // 128, 128), F32),
            zt_scratch,
            rows_scratch,
            part_scratch,
            pltpu.SemaphoreType.DMA((8,)),
            pltpu.SemaphoreType.DMA((FETCHES,)),
        ],
        megabytes=16,
        name="start",
    )
    inner = max(1, n_cam // 4)
    old_points, old_camera = (), ()
    for iteration in range(ITERS):
        first, last = iteration == 0, iteration + 1 == ITERS
        if inner > 1:
            pair = exchange(message_now, "cam", n_cam, range(1, inner))
            message_now = call(pair_kernel, message, pair, name="pair")
        parts = exchange(message_now, "cam", n_cam, range(inner, n_cam, inner))
        tile_message, point_sum, scal = call(
            functools.partial(points_kernel, len(parts), first),
            [
                shape((rows + TAIL, width), BF16),
                shape((count, 192), F32),
                shape((8, 128), F32),
            ],
            (*parts, *old_points, coupling, v6, slot),
            scratch=[pltpu.VMEM((count, cols), F32), rows_scratch],
            name="points",
        )
        old_points = (point_sum, scal)
        parts = exchange(tile_message, "pts", n_pts, range(1, n_pts))
        kernel = functools.partial(camera_kernel, len(parts), first, last)
        common = [
            pltpu.VMEM((n_pts, rows + TAIL, width), BF16),
            pltpu.VMEM((size, planes, 128), F32),
        ]
        args = (*parts, scal, z, cz, residual, *old_camera)
        if last:
            plain = shape((size, cams), F32)
            scratch = [*common, pltpu.VMEM((size, planes, 128), F32), pltpu.VMEM((8 * planes, 128), F32)]
            return tuple(call(kernel, [plain, plain], args, scratch=scratch, name="finish"))
        outs = [message, vector, vector, vector, vector] + ([] if first else [vector, vector])
        message_now, residual, solution, z_new, cz_new, *direction = call(
            kernel,
            outs,
            (*args, coupling, m4, c4, slot),
            scratch=[*common, zt_scratch, rows_scratch, part_scratch],
            name="camera",
        )
        d, cd = direction if direction else (z, cz)
        old_camera = (d, cd, solution)
        z, cz = z_new, cz_new


def solution(mesh):
    in_specs = (
        P(None, "cam"),
        P(None, None, "cam"),
        P("pts", None, "cam"),
        P(None, None, "pts"),
        P(None, None, "cam"),
        P("pts", "cam"),
        P("pts", "cam"),
    )
    out_specs = (P(None, "cam"), P(None, "cam"))
    return jax.shard_map(
        functools.partial(per_device, mesh.shape["cam"], mesh.shape["pts"]),
        mesh=mesh,
        in_specs=in_specs,
        out_specs=out_specs,
        check_vma=False,
    )
```

```python
import functools

import jax
import jax.numpy as jnp
from jax import lax
from jax.experimental import pallas as pl
from jax.experimental.pallas import tpu as pltpu
from jax.sharding import PartitionSpec as P


ITERS = 3
F32 = jnp.float32
BF16 = jnp.bfloat16
VMEM = pl.BlockSpec(memory_space=pltpu.VMEM)
HBM = pl.BlockSpec(memory_space=pltpu.HBM)
NT = (((1,), (1,)), ((), ()))
FETCHES = 4
TAIL = 8
BACKWARD_SHARE = 7


def in_hbm(value):
    return pltpu.with_memory_space_constraint(value, pltpu.HBM)


def iota(shape, dim):
    return lax.broadcasted_iota(jnp.int32, shape, dim)


def tree_sum(values):
    while len(values) > 1:
        values = [a + b for a, b in zip(values[::2], values[1::2])] + values[
            len(values) - len(values) % 2 :
        ]
    return values[0]


def sym(size, i, j):
    i, j = min(i, j), max(i, j)
    return i * size - i * (i - 1) // 2 + (j - i)


def total(value):
    return jnp.sum(value, keepdims=True)


def pieces(value):
    high = value.astype(BF16).astype(F32)
    rest = value - high
    middle = rest.astype(BF16).astype(F32)
    return [high, middle, rest - middle]


def scalar_lanes(scalars, rows):
    lane = iota((rows, 64), 1)
    tile = jnp.zeros((rows, 64), F32)
    for at, piece in enumerate(p for s in scalars for p in pieces(s)):
        tile = jnp.where(lane == at, piece, tile)
    return tile


def read_scalars(tile, count):
    row = tile[0:1, :]
    return [
        row[:, 3 * n : 3 * n + 1] + row[:, 3 * n + 1 : 3 * n + 2] + row[:, 3 * n + 2 : 3 * n + 3]
        for n in range(count)
    ]


def sym_rows(matrix, size, rows, vector):
    return [
        tree_sum([matrix[sym(size, i, j), rows, :] * vector[j] for j in range(size)])
        for i in range(size)
    ]


def tile_onehot(rows, tiles, planes):
    row_a, row_q = rows[0:1, :], rows[1:2, :]
    at = jnp.where(row_a >= 0, row_q * planes + row_a, -1.0).astype(jnp.int32)
    return jnp.where(iota((tiles, at.shape[1]), 0) == at, 1.0, 0.0).astype(BF16)


def to_tiles(z_ref, zt_ref):
    planes = z_ref.shape[1]
    for j in range(z_ref.shape[0]):
        turned = z_ref[j].T
        parts = [turned[16 * q : 16 * q + 16, :] for q in range(8)]
        zt_ref[16 * j : 16 * j + 16, :] = jnp.concatenate(parts, axis=1).astype(BF16)


def from_tiles(tiles, t4_ref):
    planes = t4_ref.shape[1]
    for j in range(t4_ref.shape[0]):
        block = tiles[16 * j : 16 * j + 16, :]
        parts = [block[:, q * planes : (q + 1) * planes] for q in range(8)]
        t4_ref[j] = jnp.concatenate(parts, axis=0).T


def gather_rows(zt_ref, onehot, rows_ref):
    rows_ref[...] = jnp.dot(zt_ref[...], onehot, preferred_element_type=F32).T


def on_vector_unit(pair, share):
    return (pair + 1) * share // 16 > pair * share // 16


def forward_pairs(e_ref, rows_ref, part_ref, pairs):
    sub = iota((8, rows_ref.shape[1]), 0)
    for pair in pairs:
        at = pl.ds(8 * pair, 8)
        both = rows_ref[at, :]
        top = jnp.where(sub < 4, both, 0.0).astype(BF16)
        low = jnp.where(sub >= 4, both, 0.0).astype(BF16)
        part = jnp.dot(top, e_ref[2 * pair], preferred_element_type=F32) + jnp.dot(
            low, e_ref[2 * pair + 1], preferred_element_type=F32
        )
        for i in range(part_ref.shape[0]):
            part_ref[i, at, :] = part[:, 128 * i : 128 * i + 128]


def forward_sum(part_ref, count):
    def pick(i, s):
        return part_ref[i, pl.ds(s, count, 4), :]

    even = jnp.concatenate([pick(0, 0) + pick(3, 2), pick(1, 0) + pick(4, 2)], axis=1)
    odd = jnp.concatenate([pick(1, 1) + pick(4, 3), pick(2, 1) + pick(5, 3)], axis=1)
    return even[:, :192] + odd[:, 64:]


def backward(e_ref, y, yc_ref, rows_ref, cols_ref):
    count, rows = e_ref.shape[:2]
    wide = [jnp.concatenate(pair, axis=1) for pair in ((y[0], y[1]), (y[2], y[0]), (y[1], y[2]))]
    for i in range(6):
        yc_ref[:, 128 * i : 128 * i + 128] = wide[i % 3]
    row, col = iota((8, 768), 0), iota((8, 768), 1)
    masks = [(col >= 192 * (row - r)) & (col < 192 * (row - r) + 192) for r in (0, 4)]
    low_lanes = iota((1, 128), 1) < 64
    for pair in range(count // 2):
        if on_vector_unit(pair, BACKWARD_SHARE):
            for t in (2 * pair, 2 * pair + 1):
                e = [e_ref[t, :, 128 * i : 128 * i + 128].astype(F32) for i in range(6)]
                w = [yc_ref[pl.ds(t, 1), 128 * i : 128 * i + 128] for i in range(3)]
                w_low, w_high = jnp.where(low_lanes, w[1], 0.0), jnp.where(low_lanes, 0.0, w[1])
                sums = (
                    e[0] * w[0] + e[1] * w_low,
                    e[1] * w_high + e[2] * w[2],
                    e[3] * w[0] + e[4] * w_low,
                    e[4] * w_high + e[5] * w[2],
                )
                for s, value in enumerate(sums):
                    cols_ref[:, 4 * t + s : 4 * t + s + 1] = jnp.sum(value, axis=1, keepdims=True)
            continue
        part = None
        for k in range(2):
            wide_row = jnp.broadcast_to(yc_ref[pl.ds(2 * pair + k, 1), :], (8, 768))
            lhs = jnp.where(masks[k], wide_row, 0.0).astype(BF16)
            one = lax.dot_general(lhs, e_ref[2 * pair + k], NT, preferred_element_type=F32)
            part = one if part is None else part + one
        rows_ref[pl.ds(8 * pair, 8), :] = part
    pair_of = iota((rows, 4 * count), 1) // 8
    vector = on_vector_unit(pair_of, BACKWARD_SHARE)
    return jnp.where(vector, cols_ref[...], rows_ref[...].T)


def start_kernel(
    rhs_hbm, m_hbm, c_hbm, e_hbm, v_hbm, index_hbm, count_hbm,
    e_ref, m_ref, c_ref, v_ref, r_ref, z_ref, cz_ref, slot_ref, msg_ref,
    rn, mn, m8, cn, c8, vn, index_ref, count_ref, split, vrow, zt_ref, rows_ref, part_ref, sems, e_sems,
):
    planes, count = r_ref.shape[1], e_ref.shape[0]
    step = count // FETCHES
    inner = pl.ds(0, 8)

    def fetch(n):
        part = pl.ds(n * step, step)
        return pltpu.make_async_copy(e_hbm.at[part], e_ref.at[part], e_sems.at[n])

    def copy(n, src, dst):
        return pltpu.make_async_copy(src, dst, sems.at[n])

    indices = [copy(0, index_hbm, index_ref), copy(1, count_hbm, count_ref)]
    rhs = [copy(2, rhs_hbm, rn)]
    precond = [copy(3, m_hbm.at[inner, inner], mn), copy(4, m_hbm.at[8], m8)]
    camera = [copy(5, c_hbm.at[inner, inner], cn), copy(6, c_hbm.at[8], c8)]
    inverse = [copy(7, v_hbm, vn)]
    early = [fetch(n) for n in range(FETCHES // 2)]
    late = [fetch(n) for n in range(FETCHES // 2, FETCHES)]
    for one in rhs + precond + indices + early + camera + inverse + late:
        one.start()

    def wait(copies):
        for one in copies:
            one.wait()

    def split_rows(src, buffer, used):
        for a in range(src.shape[1] // 128):
            buffer[8 * a : 8 * a + used, :] = src[0:used, 128 * a : 128 * a + 128]

    def split_last(src, out_ref, at):
        for a in range(planes):
            out_ref[at, a : a + 1, :] = src[8:9, 128 * a : 128 * a + 128]

    def split_matrix(inner_ref, last_ref, out_ref):
        for i in range(9):
            buffer = split.at[i % 2]
            split_rows(inner_ref.at[i] if i < 8 else last_ref, buffer, 8)
            for j in range(i if i < 8 else 0, 8):
                out_ref[sym(9, i, j)] = buffer[pl.ds(j, planes, 8), :]
        split_last(last_ref, out_ref, sym(9, 8, 8))

    wait(rhs)
    split_rows(rn, split.at[0], 8)
    for j in range(8):
        r_ref[j] = split[0, pl.ds(j, planes, 8), :]
    split_last(rn, r_ref, 8)

    wait(indices)
    slots = index_ref.shape[0]
    width = count * slots
    index = index_ref[...]
    used = iota(index.shape, 0) < count_ref[...]
    spread = jnp.where(iota((count, width), 1) // slots == iota((count, width), 0), 1.0, 0.0)
    mine = iota((8, width), 1) % slots == iota((8, width), 0)
    pad = jnp.zeros((8 - slots, count), F32)
    slot_rows = []
    for part in (jnp.where(used, index // 8, -1), index % 8):
        padded = jnp.concatenate([part.astype(F32), pad], axis=0).astype(BF16)
        moved = jnp.dot(padded, spread.astype(BF16), preferred_element_type=F32)
        slot_rows.append(jnp.sum(jnp.where(mine, moved, 0.0), axis=0, keepdims=True))
    row = iota((8, width), 0)
    slot_ref[...] = jnp.where(row == 0, slot_rows[0], jnp.where(row == 1, slot_rows[1], 0.0))
    onehot = tile_onehot(slot_ref[...], 8 * planes, planes)

    wait(precond)
    split_matrix(mn, m8, m_ref)

    def precondition(g, inner_sum):
        rows = pl.ds(pl.multiple_of(g * 8, 8), 8)
        r = [r_ref[j, rows, :] for j in range(9)]
        z = sym_rows(m_ref, 9, rows, r)
        for j in range(9):
            z_ref[j, rows, :] = z[j]
        return inner_sum + tree_sum([a * b for a, b in zip(r, z)])

    zero = jnp.zeros((8, 128), F32)
    inner_sum = lax.fori_loop(0, planes // 8, precondition, zero, unroll=True)
    to_tiles(z_ref, zt_ref)
    gather_rows(zt_ref, onehot, rows_ref)

    def forward_chunk(n, one):
        one.wait()
        forward_pairs(e_ref, rows_ref, part_ref, range(n * step // 2, (n + 1) * step // 2))

    for n, one in enumerate(early):
        forward_chunk(n, one)

    wait(camera)
    split_matrix(cn, c8, c_ref)

    def apply_camera(g, curve):
        rows = pl.ds(pl.multiple_of(g * 8, 8), 8)
        z = [z_ref[j, rows, :] for j in range(9)]
        cz = sym_rows(c_ref, 9, rows, z)
        for j in range(9):
            cz_ref[j, rows, :] = cz[j]
        return curve + tree_sum([a * b for a, b in zip(z, cz)])

    curve = lax.fori_loop(0, planes // 8, apply_camera, zero, unroll=True)

    wait(inverse)
    half = vrow.shape[0]
    for i in range(3):
        split_rows(vn.at[i], split.at[i % 2], 3)
        for j in range(i, 3):
            plane = split[i % 2, pl.ds(j, half, 8), :]
            v_ref[sym(3, i, j), pl.ds(0, half, 2), :] = plane
            v_ref[sym(3, i, j), pl.ds(1, half, 2), :] = jnp.concatenate(
                [plane[:, 64:], plane[:, :64]], axis=1
            )

    for n, one in enumerate(late):
        forward_chunk(len(early) + n, one)
    scalars = scalar_lanes([total(inner_sum), total(curve), jnp.zeros((1, 1), F32)], count)
    msg_ref[...] = jnp.concatenate([forward_sum(part_ref, count), scalars], axis=1).astype(BF16)


def pair_kernel(*refs):
    *in_refs, out_ref = refs
    value = tree_sum([ref[...].astype(F32) for ref in in_refs])
    scalars = scalar_lanes(read_scalars(value[:, 192:], 3), value.shape[0])
    out_ref[...] = jnp.concatenate([value[:, :192], scalars], axis=1).astype(BF16)


def points_kernel(parts, first, last, *refs):
    summed = tree_sum([ref[...].astype(F32) for ref in refs[:parts]])
    refs = refs[parts:]
    if not first:
        p_old_ref, scal_old_ref, *refs = refs
    e_ref, v_ref, slot_ref, msg_ref, scal_ref, *refs = refs
    *p_out, yc_ref, c_ref, ct_ref = refs
    inner_now, z_c_z, z_c_d = read_scalars(summed[:, 192:], 3)
    point_sum = summed[:, :192]
    beta, curve = jnp.zeros((1, 1), F32), z_c_z
    if not first:
        beta = inner_now / scal_old_ref[0:1, 0:1]
        curve = z_c_z + beta * (2.0 * z_c_d + beta * scal_old_ref[1:2, 0:1])
        point_sum = point_sum + beta * p_old_ref[...]
    if not last:
        p_out[0][...] = point_sum
    row = iota((8, 128), 0)
    scal_ref[...] = jnp.where(row == 0, inner_now, jnp.where(row == 1, curve, beta))
    p = [point_sum[:, 64 * i : 64 * i + 64] for i in range(3)]
    y = [tree_sum([v_ref[sym(3, i, j)][:, :64] * p[j] for j in range(3)]) for i in range(3)]
    taken = total(tree_sum([a * b for a, b in zip(p, y)]))
    rows = c_ref.shape[1]
    msg_ref[0:rows, :] = backward(e_ref, y, yc_ref, c_ref, ct_ref).astype(BF16)
    width = msg_ref.shape[1]
    row = iota((TAIL, width), 0)
    tail = jnp.zeros((TAIL, width), F32)
    for at, value in enumerate([slot_ref[0:1, :], slot_ref[1:2, :], *pieces(taken)]):
        tail = jnp.where(row == at, value, tail)
    msg_ref[rows : rows + TAIL, :] = tail.astype(BF16)


def camera_kernel(parts, first, last, *refs):
    msgs, refs = refs[:parts], refs[parts:]
    scal_ref, z_ref, cz_ref, r_ref, *refs = refs
    if not first:
        d_old_ref, cd_old_ref, sol_old_ref, *refs = refs
    if last:
        sol_out, res_out, all_ref, t4_ref, sol_ref, split = refs
        res_ref = t4_ref
    else:
        e_ref, m_ref, c_ref, slot_ref, *refs = refs
        msg_ref, res_ref, sol_ref, zn_ref, czn_ref, *refs = refs
        if not first:
            d_ref, cd_ref, *refs = refs
        all_ref, t4_ref, zt_ref, rows_ref, part_ref = refs
    planes = z_ref.shape[1]
    rows_all = all_ref.shape[1] - TAIL
    me = lax.axis_index("pts")
    for k in range(parts):
        all_ref[me ^ k] = msgs[k][...]
    taken, tiles = [], []
    for k in range(parts):
        tail = all_ref[k, rows_all : rows_all + TAIL, :].astype(F32)
        taken.append(tail[2:3, 0:1] + tail[3:4, 0:1] + tail[4:5, 0:1])
        onehot = tile_onehot(tail, 8 * planes, planes)
        tiles.append(
            lax.dot_general(all_ref[k, 0:rows_all, :], onehot, NT, preferred_element_type=F32)
        )
    inner_now, curve, beta = scal_ref[0:1, 0:1], scal_ref[1:2, 0:1], scal_ref[2:3, 0:1]
    step_size = inner_now / (curve - tree_sum(taken))
    from_tiles(tree_sum(tiles), t4_ref)

    def update(g, sums):
        rows = pl.ds(pl.multiple_of(g * 8, 8), 8)
        r, cd = [], []
        for j in range(9):
            d, c_d = z_ref[j, rows, :], cz_ref[j, rows, :]
            if not first:
                d = d + beta * d_old_ref[j, rows, :]
                c_d = c_d + beta * cd_old_ref[j, rows, :]
                if not last:
                    d_ref[j, rows, :] = d
                    cd_ref[j, rows, :] = c_d
            step = step_size * d
            sol_ref[j, rows, :] = step if first else sol_old_ref[j, rows, :] + step
            r.append(r_ref[j, rows, :] - step_size * (c_d - t4_ref[j, rows, :]))
            cd.append(c_d)
        for j in range(9):
            res_ref[j, rows, :] = r[j]
        if last:
            return sums
        z = sym_rows(m_ref, 9, rows, r)
        cz = sym_rows(c_ref, 9, rows, z)
        for j in range(9):
            zn_ref[j, rows, :] = z[j]
            czn_ref[j, rows, :] = cz[j]
        pairs = (zip(r, z), zip(z, cz), zip(z, cd))
        return tuple(s + tree_sum([a * b for a, b in p]) for s, p in zip(sums, pairs))

    sums = lax.fori_loop(0, planes // 8, update, (jnp.zeros((8, 128), F32),) * 3, unroll=True)
    if last:
        for src, dst in ((sol_ref, sol_out), (res_ref, res_out)):
            for j in range(8):
                split[pl.ds(j, planes, 8), :] = src[j]

            def body(a, carry):
                lanes = pl.ds(pl.multiple_of(a * 128, 128), 128)
                dst[0:8, lanes] = split[pl.ds(pl.multiple_of(a * 8, 8), 8), :]
                dst[8:9, lanes] = src[8, pl.ds(a, 1), :]
                return carry

            lax.fori_loop(0, planes, body, 0, unroll=16)
        return
    to_tiles(zn_ref, zt_ref)
    onehot = tile_onehot(slot_ref[...], 8 * planes, planes)
    gather_rows(zt_ref, onehot, rows_ref)
    count = e_ref.shape[0]
    forward_pairs(e_ref, rows_ref, part_ref, range(count // 2))
    scalars = scalar_lanes([total(s) for s in sums], count)
    msg_ref[...] = jnp.concatenate([forward_sum(part_ref, count), scalars], axis=1).astype(BF16)


def per_device(n_cam, n_pts, rhs, cam_block, coupling, point_inverse, precond, tile_index, tile_count):
    count, slots = tile_index.shape
    size, cams = rhs.shape
    rows, cols = coupling.shape[1:]
    planes, tiles, width = cams // 128, cams // 16, count * slots
    points = point_inverse.shape[2]
    shape = jax.ShapeDtypeStruct
    vector = shape((size, planes, 128), F32)
    message = shape((count, 256), BF16)
    planes_of = size * (size + 1) // 2
    part_scratch = pltpu.VMEM((cols // 128, width, 128), F32)
    rows_scratch = pltpu.VMEM((width, rows), F32)
    cols_scratch = pltpu.VMEM((rows, width), F32)
    zt_scratch = pltpu.VMEM((rows, tiles), BF16)

    def call(kernel, outs, args, in_specs=None, scratch=(), megabytes=8, name=None):
        return pl.pallas_call(
            kernel,
            out_shape=outs,
            in_specs=in_specs or [VMEM] * len(args),
            out_specs=jax.tree.map(lambda _: VMEM, outs),
            scratch_shapes=list(scratch),
            compiler_params=pltpu.CompilerParams(vmem_limit_bytes=megabytes * 2**20),
            name=name,
        )(*args)

    def exchange(value, axis, axis_size, masks):
        return [value] + [
            lax.ppermute(value, axis, [(i, i ^ k) for i in range(axis_size)]) for k in masks
        ]

    coupling, m4, c4, v6, residual, z, cz, slot, message_now = call(
        start_kernel,
        [
            pltpu.VMEM(coupling.shape, BF16),
            pltpu.VMEM((planes_of, planes, 128), F32),
            pltpu.VMEM((planes_of, planes, 128), F32),
            pltpu.VMEM((6, count, 128), F32),
            vector,
            vector,
            vector,
            shape((8, width), F32),
            message,
        ],
        [
            in_hbm(value)
            for value in (
                rhs, precond, cam_block, coupling, point_inverse, tile_index.T, tile_count.T,
            )
        ],
        in_specs=[HBM] * 7,
        scratch=[
            pltpu.VMEM((size, cams), F32),
            pltpu.VMEM((8, 8, cams), F32),
            pltpu.VMEM((size, cams), F32),
            pltpu.VMEM((8, 8, cams), F32),
            pltpu.VMEM((size, cams), F32),
            pltpu.VMEM((3, 3, points), F32),
            pltpu.VMEM((slots, count), jnp.int32),
            pltpu.VMEM((1, count), jnp.int32),
            pltpu.VMEM((2, 8 * planes, 128), F32),
            pltpu.VMEM((points // 128, 128), F32),
            zt_scratch,
            rows_scratch,
            part_scratch,
            pltpu.SemaphoreType.DMA((8,)),
            pltpu.SemaphoreType.DMA((FETCHES,)),
        ],
        megabytes=16,
        name="start",
    )
    inner = max(1, n_cam // 4)
    old_points, old_camera = (), ()
    for iteration in range(ITERS):
        first, last = iteration == 0, iteration + 1 == ITERS
        if inner > 1:
            pair = exchange(message_now, "cam", n_cam, range(1, inner))
            message_now = call(pair_kernel, message, pair, name="pair")
        parts = exchange(message_now, "cam", n_cam, range(inner, n_cam, inner))
        outs = [shape((rows + TAIL, width), BF16), shape((8, 128), F32)]
        tile_message, scal, *point_sum = call(
            functools.partial(points_kernel, len(parts), first, last),
            outs + ([] if last else [shape((count, 192), F32)]),
            (*parts, *old_points, coupling, v6, slot),
            scratch=[pltpu.VMEM((count, cols), F32), rows_scratch, cols_scratch],
            name="points",
        )
        old_points = (*point_sum, scal)
        parts = exchange(tile_message, "pts", n_pts, range(1, n_pts))
        kernel = functools.partial(camera_kernel, len(parts), first, last)
        common = [
            pltpu.VMEM((n_pts, rows + TAIL, width), BF16),
            pltpu.VMEM((size, planes, 128), F32),
        ]
        args = (*parts, scal, z, cz, residual, *old_camera)
        if last:
            plain = shape((size, cams), F32)
            scratch = [*common, pltpu.VMEM((size, planes, 128), F32), pltpu.VMEM((8 * planes, 128), F32)]
            return tuple(call(kernel, [plain, plain], args, scratch=scratch, name="finish"))
        outs = [message, vector, vector, vector, vector] + ([] if first else [vector, vector])
        message_now, residual, solution, z_new, cz_new, *direction = call(
            kernel,
            outs,
            (*args, coupling, m4, c4, slot),
            scratch=[*common, zt_scratch, rows_scratch, part_scratch],
            name="camera",
        )
        d, cd = direction if direction else (z, cz)
        old_camera = (d, cd, solution)
        z, cz = z_new, cz_new


def solution(mesh):
    in_specs = (
        P(None, "cam"),
        P(None, None, "cam"),
        P("pts", None, "cam"),
        P(None, None, "pts"),
        P(None, None, "cam"),
        P("pts", "cam"),
        P("pts", "cam"),
    )
    out_specs = (P(None, "cam"), P(None, "cam"))
    return jax.shard_map(
        functools.partial(per_device, mesh.shape["cam"], mesh.shape["pts"]),
        mesh=mesh,
        in_specs=in_specs,
        out_specs=out_specs,
        check_vma=False,
    )
```

```python
import functools

import jax
import jax.numpy as jnp
from jax import lax
from jax.experimental import pallas as pl
from jax.experimental.pallas import tpu as pltpu
from jax.sharding import PartitionSpec as P


ITERS = 3
F32 = jnp.float32
BF16 = jnp.bfloat16
VMEM = pl.BlockSpec(memory_space=pltpu.VMEM)
HBM = pl.BlockSpec(memory_space=pltpu.HBM)
NT = (((1,), (1,)), ((), ()))
FETCHES = (0, 16, 40, 56, 64)
TAIL = 8
BACKWARD_SHARE = 6


def in_hbm(value):
    return pltpu.with_memory_space_constraint(value, pltpu.HBM)


def iota(shape, dim):
    return lax.broadcasted_iota(jnp.int32, shape, dim)


def tree_sum(values):
    while len(values) > 1:
        values = [a + b for a, b in zip(values[::2], values[1::2])] + values[
            len(values) - len(values) % 2 :
        ]
    return values[0]


def sym(size, i, j):
    i, j = min(i, j), max(i, j)
    return i * size - i * (i - 1) // 2 + (j - i)


def total(value):
    return jnp.sum(value, keepdims=True)


def pieces(value):
    high = value.astype(BF16).astype(F32)
    rest = value - high
    middle = rest.astype(BF16).astype(F32)
    return [high, middle, rest - middle]


def scalar_lanes(scalars, rows):
    lane = iota((rows, 64), 1)
    tile = jnp.zeros((rows, 64), F32)
    for at, piece in enumerate(p for s in scalars for p in pieces(s)):
        tile = jnp.where(lane == at, piece, tile)
    return tile


def read_scalars(tile, count):
    row = tile[0:1, :]
    number = iota(row.shape, 1) % 16 // 3
    return [total(jnp.where(number == n, row, 0.0)) for n in range(count)]


def sym_rows(matrix, size, rows, vector):
    return [
        tree_sum([matrix[sym(size, i, j), rows, :] * vector[j] for j in range(size)])
        for i in range(size)
    ]


def tile_onehot(rows, tiles, planes):
    row_a, row_q = rows[0:1, :], rows[1:2, :]
    at = jnp.where(row_a >= 0, row_q * planes + row_a, -1.0).astype(jnp.int32)
    return jnp.where(iota((tiles, at.shape[1]), 0) == at, 1.0, 0.0).astype(BF16)


def swap_halves(even, odd):
    low = iota(even.shape, 1) < 64
    return (
        jnp.where(low, even, pltpu.roll(odd, 64, 1)),
        jnp.where(low, pltpu.roll(even, 64, 1), odd),
    )


def plane_pairs(size):
    return [(j, min(j + 1, size - 1)) for j in range(0, size, 2)]


def to_tiles(z_ref, zt_ref):
    for pair in plane_pairs(z_ref.shape[0]):
        turned = jnp.concatenate([z_ref[j] for j in pair], axis=0).T
        for h in range(4):
            even, odd = (turned[16 * q : 16 * q + 16, :] for q in (2 * h, 2 * h + 1))
            for j, block in zip(pair, swap_halves(even, odd)):
                zt_ref[16 * j : 16 * j + 16, 128 * h : 128 * h + 128] = block.astype(BF16)


def from_tiles(tiles, t4_ref):
    planes = t4_ref.shape[1]
    for pair in plane_pairs(t4_ref.shape[0]):
        blocks = []
        for h in range(4):
            first, second = (
                tiles[16 * j : 16 * j + 16, 128 * h : 128 * h + 128] for j in pair
            )
            blocks += swap_halves(first, second)
        turned = jnp.concatenate(blocks, axis=0).T
        for n, j in enumerate(pair):
            t4_ref[j] = turned[n * planes : (n + 1) * planes, :]


def gather_rows(zt_ref, onehot, rows_ref):
    rows_ref[...] = jnp.dot(zt_ref[...], onehot, preferred_element_type=F32).T


def on_vector_unit(pair, share):
    return (pair + 1) * share // 16 > pair * share // 16


def forward_pairs(e_ref, rows_ref, part_ref, pairs):
    sub = iota((8, rows_ref.shape[1]), 0)
    for pair in pairs:
        at = pl.ds(8 * pair, 8)
        both = rows_ref[at, :]
        top = jnp.where(sub < 4, both, 0.0).astype(BF16)
        low = jnp.where(sub >= 4, both, 0.0).astype(BF16)
        part = jnp.dot(top, e_ref[2 * pair], preferred_element_type=F32) + jnp.dot(
            low, e_ref[2 * pair + 1], preferred_element_type=F32
        )
        for i in range(part_ref.shape[0]):
            part_ref[i, at, :] = part[:, 128 * i : 128 * i + 128]


def forward_sum(part_ref, count):
    def pick(i, s):
        return part_ref[i, pl.ds(s, count, 4), :]

    even = jnp.concatenate([pick(0, 0) + pick(3, 2), pick(1, 0) + pick(4, 2)], axis=1)
    odd = jnp.concatenate([pick(1, 1) + pick(4, 3), pick(2, 1) + pick(5, 3)], axis=1)
    return even[:, :192] + odd[:, 64:]


def backward(e_ref, y, yc_ref, rows_ref, cols_ref):
    count, rows = e_ref.shape[:2]
    wide = [jnp.concatenate(pair, axis=1) for pair in ((y[0], y[1]), (y[2], y[0]), (y[1], y[2]))]
    for i in range(6):
        yc_ref[:, 128 * i : 128 * i + 128] = wide[i % 3]
    row, col = iota((8, 768), 0), iota((8, 768), 1)
    masks = [(col >= 192 * (row - r)) & (col < 192 * (row - r) + 192) for r in (0, 4)]
    low_lanes = iota((1, 128), 1) < 64
    for pair in range(count // 2):
        if on_vector_unit(pair, BACKWARD_SHARE):
            for t in (2 * pair, 2 * pair + 1):
                e = [e_ref[t, :, 128 * i : 128 * i + 128].astype(F32) for i in range(6)]
                w = [yc_ref[pl.ds(t, 1), 128 * i : 128 * i + 128] for i in range(3)]
                w_low, w_high = jnp.where(low_lanes, w[1], 0.0), jnp.where(low_lanes, 0.0, w[1])
                sums = (
                    e[0] * w[0] + e[1] * w_low,
                    e[1] * w_high + e[2] * w[2],
                    e[3] * w[0] + e[4] * w_low,
                    e[4] * w_high + e[5] * w[2],
                )
                for s, value in enumerate(sums):
                    cols_ref[:, 4 * t + s : 4 * t + s + 1] = jnp.sum(value, axis=1, keepdims=True)
            continue
        part = None
        for k in range(2):
            wide_row = jnp.broadcast_to(yc_ref[pl.ds(2 * pair + k, 1), :], (8, 768))
            lhs = jnp.where(masks[k], wide_row, 0.0).astype(BF16)
            one = lax.dot_general(lhs, e_ref[2 * pair + k], NT, preferred_element_type=F32)
            part = one if part is None else part + one
        rows_ref[pl.ds(8 * pair, 8), :] = part
    pair_of = iota((rows, 4 * count), 1) // 8
    vector = on_vector_unit(pair_of, BACKWARD_SHARE)
    return jnp.where(vector, cols_ref[...], rows_ref[...].T)


def start_kernel(
    rhs_hbm, m_hbm, c_hbm, e_hbm, v_hbm, index_hbm, count_hbm,
    e_ref, m_ref, c_ref, v_ref, r_ref, z_ref, cz_ref, slot_ref, msg_ref,
    rn, mn, m8, cn, c8, vn, index_ref, count_ref, split, vrow, zt_ref, rows_ref, part_ref, sems, e_sems,
):
    planes, count = r_ref.shape[1], e_ref.shape[0]
    ends = [count * end // 64 for end in FETCHES]
    parts = list(zip(ends[:-1], ends[1:]))
    inner = pl.ds(0, 8)

    def fetch(n):
        part = pl.ds(parts[n][0], parts[n][1] - parts[n][0])
        return pltpu.make_async_copy(e_hbm.at[part], e_ref.at[part], e_sems.at[n])

    def copy(n, src, dst):
        return pltpu.make_async_copy(src, dst, sems.at[n])

    indices = [copy(0, index_hbm, index_ref), copy(1, count_hbm, count_ref)]
    rhs = [copy(2, rhs_hbm, rn)]
    precond = [copy(3, m_hbm.at[inner, inner], mn), copy(4, m_hbm.at[8], m8)]
    camera = [copy(5, c_hbm.at[inner, inner], cn), copy(6, c_hbm.at[8], c8)]
    inverse = [copy(7, v_hbm, vn)]
    early = [fetch(n) for n in range(2)]
    late = [fetch(n) for n in range(2, len(parts))]
    for one in rhs + precond + indices + early + camera + inverse + late:
        one.start()

    def wait(copies):
        for one in copies:
            one.wait()

    def split_rows(src, buffer, used):
        for a in range(src.shape[1] // 128):
            buffer[8 * a : 8 * a + used, :] = src[0:used, 128 * a : 128 * a + 128]

    def split_last(src, out_ref, at):
        for a in range(planes):
            out_ref[at, a : a + 1, :] = src[8:9, 128 * a : 128 * a + 128]

    def split_matrix(inner_ref, last_ref, out_ref):
        for i in range(9):
            buffer = split.at[i % 2]
            split_rows(inner_ref.at[i] if i < 8 else last_ref, buffer, 8)
            for j in range(i if i < 8 else 0, 8):
                out_ref[sym(9, i, j)] = buffer[pl.ds(j, planes, 8), :]
        split_last(last_ref, out_ref, sym(9, 8, 8))

    wait(rhs)
    split_rows(rn, split.at[0], 8)
    for j in range(8):
        r_ref[j] = split[0, pl.ds(j, planes, 8), :]
    split_last(rn, r_ref, 8)

    wait(indices)
    slots = index_ref.shape[0]
    width = count * slots
    index = index_ref[...]
    used = iota(index.shape, 0) < count_ref[...]
    spread = jnp.where(iota((count, width), 1) // slots == iota((count, width), 0), 1.0, 0.0)
    mine = iota((8, width), 1) % slots == iota((8, width), 0)
    pad = jnp.zeros((8 - slots, count), F32)
    slot_rows = []
    for part in (jnp.where(used, index // 8, -1), index % 8):
        padded = jnp.concatenate([part.astype(F32), pad], axis=0).astype(BF16)
        moved = jnp.dot(padded, spread.astype(BF16), preferred_element_type=F32)
        slot_rows.append(jnp.sum(jnp.where(mine, moved, 0.0), axis=0, keepdims=True))
    row = iota((8, width), 0)
    slot_ref[...] = jnp.where(row == 0, slot_rows[0], jnp.where(row == 1, slot_rows[1], 0.0))
    onehot = tile_onehot(slot_ref[...], 8 * planes, planes)

    wait(precond)
    split_matrix(mn, m8, m_ref)

    def precondition(g, inner_sum):
        rows = pl.ds(pl.multiple_of(g * 8, 8), 8)
        r = [r_ref[j, rows, :] for j in range(9)]
        z = sym_rows(m_ref, 9, rows, r)
        for j in range(9):
            z_ref[j, rows, :] = z[j]
        return inner_sum + tree_sum([a * b for a, b in zip(r, z)])

    zero = jnp.zeros((8, 128), F32)
    inner_sum = lax.fori_loop(0, planes // 8, precondition, zero, unroll=True)
    to_tiles(z_ref, zt_ref)
    gather_rows(zt_ref, onehot, rows_ref)

    def forward_chunk(n, one):
        one.wait()
        forward_pairs(e_ref, rows_ref, part_ref, range(parts[n][0] // 2, parts[n][1] // 2))

    for n, one in enumerate(early):
        forward_chunk(n, one)

    wait(camera)
    split_matrix(cn, c8, c_ref)

    def apply_camera(g, curve):
        rows = pl.ds(pl.multiple_of(g * 8, 8), 8)
        z = [z_ref[j, rows, :] for j in range(9)]
        cz = sym_rows(c_ref, 9, rows, z)
        for j in range(9):
            cz_ref[j, rows, :] = cz[j]
        return curve + tree_sum([a * b for a, b in zip(z, cz)])

    curve = lax.fori_loop(0, planes // 8, apply_camera, zero, unroll=True)

    wait(inverse)
    half = vrow.shape[0]
    for i in range(3):
        split_rows(vn.at[i], split.at[i % 2], 3)
        for j in range(i, 3):
            plane = split[i % 2, pl.ds(j, half, 8), :]
            v_ref[sym(3, i, j), pl.ds(0, half, 2), :] = plane
            v_ref[sym(3, i, j), pl.ds(1, half, 2), :] = jnp.concatenate(
                [plane[:, 64:], plane[:, :64]], axis=1
            )

    for n, one in enumerate(late):
        forward_chunk(len(early) + n, one)
    scalars = scalar_lanes([total(inner_sum), total(curve), jnp.zeros((1, 1), F32)], count)
    msg_ref[...] = jnp.concatenate([forward_sum(part_ref, count), scalars], axis=1).astype(BF16)


def pair_kernel(*refs):
    *in_refs, out_ref = refs
    values = [ref[...].astype(F32) for ref in in_refs]
    scalars = []
    for k, value in enumerate(values):
        lanes = value[:, 192:]
        if k > 0:
            lanes = jnp.concatenate([lanes[:, 64 - 16 * k :], lanes[:, : 64 - 16 * k]], axis=1)
        scalars.append(lanes)
    points = tree_sum([value[:, :192] for value in values])
    out_ref[...] = jnp.concatenate([points, tree_sum(scalars)], axis=1).astype(BF16)


def points_kernel(parts, first, last, *refs):
    summed = tree_sum([ref[...].astype(F32) for ref in refs[:parts]])
    refs = refs[parts:]
    if not first:
        scal_old_ref, y_old_ref, ct_old_ref, *refs = refs
    e_ref, v_ref, slot_ref, msg_ref, scal_ref, *refs = refs
    *kept, yc_ref, c_ref, ct_ref = refs
    inner_now, z_c_z, z_c_d = read_scalars(summed[:, 192:], 3)
    beta, curve = jnp.zeros((1, 1), F32), z_c_z
    if not first:
        beta = inner_now / scal_old_ref[0:1, 0:1]
        curve = z_c_z + beta * (2.0 * z_c_d + beta * scal_old_ref[1:2, 0:1])
    p = [summed[:, 64 * i : 64 * i + 64] for i in range(3)]
    y = [tree_sum([v_ref[sym(3, i, j)][:, :64] * p[j] for j in range(3)]) for i in range(3)]
    taken = total(tree_sum([a * b for a, b in zip(p, y)]))
    ct = backward(e_ref, y, yc_ref, c_ref, ct_ref)
    if not first:
        crossed = total(tree_sum([p[i] * y_old_ref[i] for i in range(3)]))
        taken = taken + beta * (2.0 * crossed + beta * scal_old_ref[3:4, 0:1])
        ct = ct + beta * ct_old_ref[...]
        y = [y[i] + beta * y_old_ref[i] for i in range(3)]
    if not last:
        y_ref, ct_out_ref = kept
        for i in range(3):
            y_ref[i] = y[i]
        ct_out_ref[...] = ct
    row = iota((8, 128), 0)
    scal = jnp.where(row == 0, inner_now, jnp.where(row == 1, curve, beta))
    scal_ref[...] = jnp.where(row == 3, taken, scal)
    rows, width = ct.shape
    msg_ref[0:rows, :] = ct.astype(BF16)
    row = iota((TAIL, width), 0)
    tail = jnp.zeros((TAIL, width), F32)
    for at, value in enumerate([slot_ref[0:1, :], slot_ref[1:2, :], *pieces(taken)]):
        tail = jnp.where(row == at, value, tail)
    msg_ref[rows : rows + TAIL, :] = tail.astype(BF16)


def camera_kernel(masks, first, last, *refs):
    parts = len(masks)
    msgs, refs = refs[:parts], refs[parts:]
    scal_ref, z_ref, cz_ref, r_ref, *refs = refs
    if not first:
        d_old_ref, cd_old_ref, sol_old_ref, *refs = refs
    if last:
        sol_hbm, res_hbm, all_ref, t4_ref, sol_ref, split, sol_out, res_out, sems = refs
    else:
        e_ref, m_ref, c_ref, slot_ref, *refs = refs
        msg_ref, res_ref, sol_ref, zn_ref, czn_ref, *refs = refs
        if not first:
            d_ref, cd_ref, *refs = refs
        all_ref, t4_ref, zt_ref, rows_ref, part_ref = refs
    planes = z_ref.shape[1]
    rows_all = all_ref.shape[1] - TAIL
    me = lax.axis_index("pts")
    for mask, msg in zip(masks, msgs):
        all_ref[me ^ mask] = msg[...]
    taken, tiles = [], []
    for k in range(parts):
        tail = all_ref[k, rows_all : rows_all + TAIL, :].astype(F32)
        taken.append(tail[2:3, 0:1] + tail[3:4, 0:1] + tail[4:5, 0:1])
        onehot = tile_onehot(tail, 8 * planes, planes)
        tiles.append(
            lax.dot_general(all_ref[k, 0:rows_all, :], onehot, NT, preferred_element_type=F32)
        )
    inner_now, curve, beta = scal_ref[0:1, 0:1], scal_ref[1:2, 0:1], scal_ref[2:3, 0:1]
    step_size = inner_now / (curve - tree_sum(taken))
    from_tiles(tree_sum(tiles), t4_ref)

    def update_last(g, carry):
        rows = pl.ds(pl.multiple_of(g * 8, 8), 8)
        for j in range(9):
            d = z_ref[j, rows, :] + beta * d_old_ref[j, rows, :]
            c_d = cz_ref[j, rows, :] + beta * cd_old_ref[j, rows, :]
            sol_ref[j, rows, :] = sol_old_ref[j, rows, :] + step_size * d
            t4_ref[j, rows, :] = r_ref[j, rows, :] - step_size * (c_d - t4_ref[j, rows, :])
        return carry

    def write(n, src, wide, dst):
        buffer = split.at[n]
        for j in range(8):
            buffer[pl.ds(j, planes, 8), :] = src[j]
        for a in range(planes):
            wide[0:8, 128 * a : 128 * a + 128] = buffer[8 * a : 8 * a + 8, :]
            wide[8:9, 128 * a : 128 * a + 128] = src[8, a : a + 1, :]
        copy = pltpu.make_async_copy(wide, dst, sems.at[n])
        copy.start()
        return copy

    if last:
        lax.fori_loop(0, planes // 8, update_last, 0, unroll=True)
        copies = [write(0, sol_ref, sol_out, sol_hbm), write(1, t4_ref, res_out, res_hbm)]
        for copy in copies:
            copy.wait()
        return

    def update(g, sums):
        rows = pl.ds(pl.multiple_of(g * 8, 8), 8)
        r, cd = [], []
        for j in range(9):
            d, c_d = z_ref[j, rows, :], cz_ref[j, rows, :]
            if not first:
                d = d + beta * d_old_ref[j, rows, :]
                c_d = c_d + beta * cd_old_ref[j, rows, :]
                d_ref[j, rows, :] = d
                cd_ref[j, rows, :] = c_d
            step = step_size * d
            sol_ref[j, rows, :] = step if first else sol_old_ref[j, rows, :] + step
            r.append(r_ref[j, rows, :] - step_size * (c_d - t4_ref[j, rows, :]))
            cd.append(c_d)
        for j in range(9):
            res_ref[j, rows, :] = r[j]
        z = sym_rows(m_ref, 9, rows, r)
        cz = sym_rows(c_ref, 9, rows, z)
        for j in range(9):
            zn_ref[j, rows, :] = z[j]
            czn_ref[j, rows, :] = cz[j]
        pairs = (zip(r, z), zip(z, cz), zip(z, cd))
        return tuple(s + tree_sum([a * b for a, b in p]) for s, p in zip(sums, pairs))

    sums = lax.fori_loop(0, planes // 8, update, (jnp.zeros((8, 128), F32),) * 3, unroll=True)
    to_tiles(zn_ref, zt_ref)
    onehot = tile_onehot(slot_ref[...], 8 * planes, planes)
    gather_rows(zt_ref, onehot, rows_ref)
    count = e_ref.shape[0]
    forward_pairs(e_ref, rows_ref, part_ref, range(count // 2))
    scalars = scalar_lanes([total(s) for s in sums], count)
    msg_ref[...] = jnp.concatenate([forward_sum(part_ref, count), scalars], axis=1).astype(BF16)


def per_device(n_cam, n_pts, rhs, cam_block, coupling, point_inverse, precond, tile_index, tile_count):
    count, slots = tile_index.shape
    size, cams = rhs.shape
    rows, cols = coupling.shape[1:]
    planes, tiles, width = cams // 128, cams // 16, count * slots
    points = point_inverse.shape[2]
    shape = jax.ShapeDtypeStruct
    vector = shape((size, planes, 128), F32)
    message = shape((count, 256), BF16)
    planes_of = size * (size + 1) // 2
    part_scratch = pltpu.VMEM((cols // 128, width, 128), F32)
    rows_scratch = pltpu.VMEM((width, rows), F32)
    cols_scratch = pltpu.VMEM((rows, width), F32)
    zt_scratch = pltpu.VMEM((rows, tiles), BF16)

    def call(kernel, outs, args, in_specs=None, scratch=(), megabytes=8, out_spec=VMEM, name=None):
        return pl.pallas_call(
            kernel,
            out_shape=outs,
            in_specs=in_specs or [VMEM] * len(args),
            out_specs=jax.tree.map(lambda _: out_spec, outs),
            scratch_shapes=list(scratch),
            compiler_params=pltpu.CompilerParams(vmem_limit_bytes=megabytes * 2**20),
            name=name,
        )(*args)

    def exchange(value, axis, axis_size, masks):
        return [value] + [
            lax.ppermute(value, axis, [(i, i ^ k) for i in range(axis_size)]) for k in masks
        ]

    coupling, m4, c4, v6, residual, z, cz, slot, message_now = call(
        start_kernel,
        [
            pltpu.VMEM(coupling.shape, BF16),
            pltpu.VMEM((planes_of, planes, 128), F32),
            pltpu.VMEM((planes_of, planes, 128), F32),
            pltpu.VMEM((6, count, 128), F32),
            vector,
            vector,
            vector,
            shape((8, width), F32),
            message,
        ],
        [
            in_hbm(value)
            for value in (
                rhs, precond, cam_block, coupling, point_inverse, tile_index.T, tile_count.T,
            )
        ],
        in_specs=[HBM] * 7,
        scratch=[
            pltpu.VMEM((size, cams), F32),
            pltpu.VMEM((8, 8, cams), F32),
            pltpu.VMEM((size, cams), F32),
            pltpu.VMEM((8, 8, cams), F32),
            pltpu.VMEM((size, cams), F32),
            pltpu.VMEM((3, 3, points), F32),
            pltpu.VMEM((slots, count), jnp.int32),
            pltpu.VMEM((1, count), jnp.int32),
            pltpu.VMEM((2, 8 * planes, 128), F32),
            pltpu.VMEM((points // 128, 128), F32),
            zt_scratch,
            rows_scratch,
            part_scratch,
            pltpu.SemaphoreType.DMA((8,)),
            pltpu.SemaphoreType.DMA((len(FETCHES) - 1,)),
        ],
        megabytes=16,
        name="start",
    )
    inner = max(1, n_cam // 4)
    old_points, old_camera = (), ()
    for iteration in range(ITERS):
        first, last = iteration == 0, iteration + 1 == ITERS
        if inner > 1:
            pair = exchange(message_now, "cam", n_cam, range(1, inner))
            message_now = call(pair_kernel, message, pair, name="pair")
        parts = exchange(message_now, "cam", n_cam, range(inner, n_cam, inner))
        outs = [shape((rows + TAIL, width), BF16), shape((8, 128), F32)]
        kept = [] if last else [shape((3, count, 64), F32), shape((rows, width), F32)]
        tile_message, scal, *kept = call(
            functools.partial(points_kernel, len(parts), first, last),
            outs + kept,
            (*parts, *old_points, coupling, v6, slot),
            scratch=[pltpu.VMEM((count, cols), F32), rows_scratch, cols_scratch],
            name="points",
        )
        old_points = (scal, *kept)
        masks = (*range(1, n_pts, 2), *range(2, n_pts, 2))
        parts = exchange(tile_message, "pts", n_pts, masks)
        kernel = functools.partial(camera_kernel, (0, *masks), first, last)
        common = [
            pltpu.VMEM((n_pts, rows + TAIL, width), BF16),
            pltpu.VMEM((size, planes, 128), F32),
        ]
        args = (*parts, scal, z, cz, residual, *old_camera)
        if last:
            plain = shape((size, cams), F32)
            scratch = [
                *common,
                pltpu.VMEM((size, planes, 128), F32),
                pltpu.VMEM((2, 8 * planes, 128), F32),
                pltpu.VMEM((size, cams), F32),
                pltpu.VMEM((size, cams), F32),
                pltpu.SemaphoreType.DMA((2,)),
            ]
            return tuple(
                call(kernel, [plain, plain], args, scratch=scratch, out_spec=HBM, name="finish")
            )
        outs = [message, vector, vector, vector, vector] + ([] if first else [vector, vector])
        message_now, residual, solution, z_new, cz_new, *direction = call(
            kernel,
            outs,
            (*args, coupling, m4, c4, slot),
            scratch=[*common, zt_scratch, rows_scratch, part_scratch],
            name="camera",
        )
        d, cd = direction if direction else (z, cz)
        old_camera = (d, cd, solution)
        z, cz = z_new, cz_new


def solution(mesh):
    in_specs = (
        P(None, "cam"),
        P(None, None, "cam"),
        P("pts", None, "cam"),
        P(None, None, "pts"),
        P(None, None, "cam"),
        P("pts", "cam"),
        P("pts", "cam"),
    )
    out_specs = (P(None, "cam"), P(None, "cam"))
    return jax.shard_map(
        functools.partial(per_device, mesh.shape["cam"], mesh.shape["pts"]),
        mesh=mesh,
        in_specs=in_specs,
        out_specs=out_specs,
        check_vma=False,
    )
```

```python
import functools

import jax
import jax.numpy as jnp
from jax import lax
from jax.experimental import pallas as pl
from jax.experimental.pallas import tpu as pltpu
from jax.sharding import PartitionSpec as P


ITERS = 3
F32 = jnp.float32
BF16 = jnp.bfloat16
VMEM = pl.BlockSpec(memory_space=pltpu.VMEM)
HBM = pl.BlockSpec(memory_space=pltpu.HBM)
NT = (((1,), (1,)), ((), ()))
FETCHES = (0, 16, 40, 56, 64)
TAIL = 8
BACKWARD_SHARE = 6


def in_hbm(value):
    return pltpu.with_memory_space_constraint(value, pltpu.HBM)


def iota(shape, dim):
    return lax.broadcasted_iota(jnp.int32, shape, dim)


def tree_sum(values):
    while len(values) > 1:
        values = [a + b for a, b in zip(values[::2], values[1::2])] + values[
            len(values) - len(values) % 2 :
        ]
    return values[0]


def sym(size, i, j):
    i, j = min(i, j), max(i, j)
    return i * size - i * (i - 1) // 2 + (j - i)


def total(value):
    return jnp.sum(value, keepdims=True)


def pieces(value):
    high = value.astype(BF16).astype(F32)
    rest = value - high
    middle = rest.astype(BF16).astype(F32)
    return [high, middle, rest - middle]


def scalar_lanes(scalars, rows):
    lane = iota((rows, 64), 1)
    tile = jnp.zeros((rows, 64), F32)
    for at, piece in enumerate(p for s in scalars for p in pieces(s)):
        tile = jnp.where(lane == at, piece, tile)
    return tile


def read_scalars(tile, count):
    row = tile[0:1, :]
    number = iota(row.shape, 1) % 16 // 3
    return [total(jnp.where(number == n, row, 0.0)) for n in range(count)]


def sym_rows(matrix, size, rows, vector):
    return [
        tree_sum([matrix[sym(size, i, j), rows, :] * vector[j] for j in range(size)])
        for i in range(size)
    ]


def tile_onehot(rows, tiles, planes):
    row_a, row_q = rows[0:1, :], rows[1:2, :]
    at = jnp.where(row_a >= 0, row_q * planes + row_a, -1.0).astype(jnp.int32)
    return jnp.where(iota((tiles, at.shape[1]), 0) == at, 1.0, 0.0).astype(BF16)


def swap_halves(even, odd):
    low = iota(even.shape, 1) < 64
    return (
        jnp.where(low, even, pltpu.roll(odd, 64, 1)),
        jnp.where(low, pltpu.roll(even, 64, 1), odd),
    )


def plane_pairs(size):
    return [(j, min(j + 1, size - 1)) for j in range(0, size, 2)]


def to_tiles(z_ref, zt_ref):
    for pair in plane_pairs(z_ref.shape[0]):
        turned = jnp.concatenate([z_ref[j] for j in pair], axis=0).T
        for h in range(4):
            even, odd = (turned[16 * q : 16 * q + 16, :] for q in (2 * h, 2 * h + 1))
            for j, block in zip(pair, swap_halves(even, odd)):
                zt_ref[16 * j : 16 * j + 16, 128 * h : 128 * h + 128] = block.astype(BF16)


def from_tiles(tiles, t4_ref):
    planes = t4_ref.shape[1]
    for pair in plane_pairs(t4_ref.shape[0]):
        blocks = []
        for h in range(4):
            first, second = (
                tiles[16 * j : 16 * j + 16, 128 * h : 128 * h + 128] for j in pair
            )
            blocks += swap_halves(first, second)
        turned = jnp.concatenate(blocks, axis=0).T
        for n, j in enumerate(pair):
            t4_ref[j] = turned[n * planes : (n + 1) * planes, :]


def gather_rows(zt_ref, onehot, rows_ref):
    rows_ref[...] = jnp.dot(zt_ref[...], onehot, preferred_element_type=F32).T


def on_vector_unit(pair, share):
    return (pair + 1) * share // 16 > pair * share // 16


def forward_pairs(e_ref, rows_ref, part_ref, pairs):
    sub = iota((8, rows_ref.shape[1]), 0)
    for pair in pairs:
        at = pl.ds(8 * pair, 8)
        both = rows_ref[at, :]
        top = jnp.where(sub < 4, both, 0.0).astype(BF16)
        low = jnp.where(sub >= 4, both, 0.0).astype(BF16)
        part = jnp.dot(top, e_ref[2 * pair], preferred_element_type=F32) + jnp.dot(
            low, e_ref[2 * pair + 1], preferred_element_type=F32
        )
        for i in range(part_ref.shape[0]):
            part_ref[i, at, :] = part[:, 128 * i : 128 * i + 128]


def forward_sum(part_ref, count):
    def pick(i, s):
        return part_ref[i, pl.ds(s, count, 4), :]

    even = jnp.concatenate([pick(0, 0) + pick(3, 2), pick(1, 0) + pick(4, 2)], axis=1)
    odd = jnp.concatenate([pick(1, 1) + pick(4, 3), pick(2, 1) + pick(5, 3)], axis=1)
    return even[:, :192] + odd[:, 64:]


def backward(e_ref, y, yc_ref, rows_ref, cols_ref):
    count, rows = e_ref.shape[:2]
    wide = [jnp.concatenate(pair, axis=1) for pair in ((y[0], y[1]), (y[2], y[0]), (y[1], y[2]))]
    for i in range(6):
        yc_ref[:, 128 * i : 128 * i + 128] = wide[i % 3]
    row, col = iota((8, 768), 0), iota((8, 768), 1)
    masks = [(col >= 192 * (row - r)) & (col < 192 * (row - r) + 192) for r in (0, 4)]
    low_lanes = iota((1, 128), 1) < 64
    for pair in range(count // 2):
        if on_vector_unit(pair, BACKWARD_SHARE):
            for t in (2 * pair, 2 * pair + 1):
                e = [e_ref[t, :, 128 * i : 128 * i + 128].astype(F32) for i in range(6)]
                w = [yc_ref[pl.ds(t, 1), 128 * i : 128 * i + 128] for i in range(3)]
                w_low, w_high = jnp.where(low_lanes, w[1], 0.0), jnp.where(low_lanes, 0.0, w[1])
                sums = (
                    e[0] * w[0] + e[1] * w_low,
                    e[1] * w_high + e[2] * w[2],
                    e[3] * w[0] + e[4] * w_low,
                    e[4] * w_high + e[5] * w[2],
                )
                for s, value in enumerate(sums):
                    cols_ref[:, 4 * t + s : 4 * t + s + 1] = jnp.sum(value, axis=1, keepdims=True)
            continue
        part = None
        for k in range(2):
            wide_row = jnp.broadcast_to(yc_ref[pl.ds(2 * pair + k, 1), :], (8, 768))
            lhs = jnp.where(masks[k], wide_row, 0.0).astype(BF16)
            one = lax.dot_general(lhs, e_ref[2 * pair + k], NT, preferred_element_type=F32)
            part = one if part is None else part + one
        rows_ref[pl.ds(8 * pair, 8), :] = part
    pair_of = iota((rows, 4 * count), 1) // 8
    vector = on_vector_unit(pair_of, BACKWARD_SHARE)
    return jnp.where(vector, cols_ref[...], rows_ref[...].T)


def start_kernel(
    rhs_hbm, m_hbm, c_hbm, e_hbm, v_hbm, index_hbm, count_hbm,
    e_ref, m_ref, c_ref, v_ref, r_ref, z_ref, cz_ref, slot_ref, msg_ref,
    rn, mn, m8, cn, c8, vn, index_ref, count_ref, split, vrow, zt_ref, rows_ref, part_ref, sems, e_sems,
):
    planes, count = r_ref.shape[1], e_ref.shape[0]
    ends = [count * end // 64 for end in FETCHES]
    parts = list(zip(ends[:-1], ends[1:]))
    inner = pl.ds(0, 8)

    def fetch(n):
        part = pl.ds(parts[n][0], parts[n][1] - parts[n][0])
        return pltpu.make_async_copy(e_hbm.at[part], e_ref.at[part], e_sems.at[n])

    def copy(n, src, dst):
        return pltpu.make_async_copy(src, dst, sems.at[n])

    indices = [copy(0, index_hbm, index_ref), copy(1, count_hbm, count_ref)]
    rhs = [copy(2, rhs_hbm, rn)]
    precond = [copy(3, m_hbm.at[inner, inner], mn), copy(4, m_hbm.at[8], m8)]
    camera = [copy(5, c_hbm.at[inner, inner], cn), copy(6, c_hbm.at[8], c8)]
    inverse = [copy(7, v_hbm, vn)]
    early = [fetch(n) for n in range(2)]
    late = [fetch(n) for n in range(2, len(parts))]
    for one in rhs + precond + indices + early + camera + inverse + late:
        one.start()

    def wait(copies):
        for one in copies:
            one.wait()

    def split_rows(src, buffer, used):
        for a in range(src.shape[1] // 128):
            buffer[8 * a : 8 * a + used, :] = src[0:used, 128 * a : 128 * a + 128]

    def split_last(src, out_ref, at):
        for a in range(planes):
            out_ref[at, a : a + 1, :] = src[8:9, 128 * a : 128 * a + 128]

    def split_matrix(inner_ref, last_ref, out_ref):
        for i in range(9):
            buffer = split.at[i % 2]
            split_rows(inner_ref.at[i] if i < 8 else last_ref, buffer, 8)
            for j in range(i if i < 8 else 0, 8):
                out_ref[sym(9, i, j)] = buffer[pl.ds(j, planes, 8), :]
        split_last(last_ref, out_ref, sym(9, 8, 8))

    wait(rhs)
    split_rows(rn, split.at[0], 8)
    for j in range(8):
        r_ref[j] = split[0, pl.ds(j, planes, 8), :]
    split_last(rn, r_ref, 8)

    wait(indices)
    slots = index_ref.shape[0]
    width = count * slots
    index = index_ref[...]
    used = iota(index.shape, 0) < count_ref[...]
    spread = jnp.where(iota((count, width), 1) // slots == iota((count, width), 0), 1.0, 0.0)
    mine = iota((8, width), 1) % slots == iota((8, width), 0)
    pad = jnp.zeros((8 - slots, count), F32)
    slot_rows = []
    for part in (jnp.where(used, index // 8, -1), index % 8):
        padded = jnp.concatenate([part.astype(F32), pad], axis=0).astype(BF16)
        moved = jnp.dot(padded, spread.astype(BF16), preferred_element_type=F32)
        slot_rows.append(jnp.sum(jnp.where(mine, moved, 0.0), axis=0, keepdims=True))
    row = iota((8, width), 0)
    slot_ref[...] = jnp.where(row == 0, slot_rows[0], jnp.where(row == 1, slot_rows[1], 0.0))
    onehot = tile_onehot(slot_ref[...], 8 * planes, planes)

    wait(precond)
    split_matrix(mn, m8, m_ref)

    def precondition(g, inner_sum):
        rows = pl.ds(pl.multiple_of(g * 8, 8), 8)
        r = [r_ref[j, rows, :] for j in range(9)]
        z = sym_rows(m_ref, 9, rows, r)
        for j in range(9):
            z_ref[j, rows, :] = z[j]
        return inner_sum + tree_sum([a * b for a, b in zip(r, z)])

    zero = jnp.zeros((8, 128), F32)
    inner_sum = lax.fori_loop(0, planes // 8, precondition, zero, unroll=True)
    to_tiles(z_ref, zt_ref)
    gather_rows(zt_ref, onehot, rows_ref)

    def forward_chunk(n, one):
        one.wait()
        forward_pairs(e_ref, rows_ref, part_ref, range(parts[n][0] // 2, parts[n][1] // 2))

    for n, one in enumerate(early):
        forward_chunk(n, one)

    wait(camera)
    split_matrix(cn, c8, c_ref)

    def apply_camera(g, curve):
        rows = pl.ds(pl.multiple_of(g * 8, 8), 8)
        z = [z_ref[j, rows, :] for j in range(9)]
        cz = sym_rows(c_ref, 9, rows, z)
        for j in range(9):
            cz_ref[j, rows, :] = cz[j]
        return curve + tree_sum([a * b for a, b in zip(z, cz)])

    curve = lax.fori_loop(0, planes // 8, apply_camera, zero, unroll=True)

    wait(inverse)
    half = vrow.shape[0]
    for i in range(3):
        split_rows(vn.at[i], split.at[i % 2], 3)
        for j in range(i, 3):
            plane = split[i % 2, pl.ds(j, half, 8), :]
            v_ref[sym(3, i, j), pl.ds(0, half, 2), :] = plane
            v_ref[sym(3, i, j), pl.ds(1, half, 2), :] = jnp.concatenate(
                [plane[:, 64:], plane[:, :64]], axis=1
            )

    for n, one in enumerate(late):
        forward_chunk(len(early) + n, one)
    scalars = scalar_lanes([total(inner_sum), total(curve), jnp.zeros((1, 1), F32)], count)
    msg_ref[...] = jnp.concatenate([forward_sum(part_ref, count), scalars], axis=1).astype(BF16)


def pair_kernel(*refs):
    *in_refs, out_ref = refs
    values = [ref[...].astype(F32) for ref in in_refs]
    scalars = []
    for k, value in enumerate(values):
        lanes = value[:, 192:]
        if k > 0:
            lanes = jnp.concatenate([lanes[:, 64 - 16 * k :], lanes[:, : 64 - 16 * k]], axis=1)
        scalars.append(lanes)
    points = tree_sum([value[:, :192] for value in values])
    out_ref[...] = jnp.concatenate([points, tree_sum(scalars)], axis=1).astype(BF16)


def points_kernel(parts, first, last, *refs):
    summed = tree_sum([ref[...].astype(F32) for ref in refs[:parts]])
    refs = refs[parts:]
    if not first:
        scal_old_ref, y_old_ref, ct_old_ref, *refs = refs
    e_ref, v_ref, slot_ref, msg_ref, scal_ref, *refs = refs
    *kept, yc_ref, c_ref, ct_ref = refs
    inner_now, z_c_z, z_c_d = read_scalars(summed[:, 192:], 3)
    beta, curve = jnp.zeros((1, 1), F32), z_c_z
    if not first:
        beta = inner_now / scal_old_ref[0:1, 0:1]
        curve = z_c_z + beta * (2.0 * z_c_d + beta * scal_old_ref[1:2, 0:1])
    p = [summed[:, 64 * i : 64 * i + 64] for i in range(3)]
    y = [tree_sum([v_ref[sym(3, i, j)][:, :64] * p[j] for j in range(3)]) for i in range(3)]
    taken = total(tree_sum([a * b for a, b in zip(p, y)]))
    ct = backward(e_ref, y, yc_ref, c_ref, ct_ref)
    if not first:
        crossed = total(tree_sum([p[i] * y_old_ref[i] for i in range(3)]))
        taken = taken + beta * (2.0 * crossed + beta * scal_old_ref[3:4, 0:1])
        ct = ct + beta * ct_old_ref[...]
        y = [y[i] + beta * y_old_ref[i] for i in range(3)]
    if not last:
        y_ref, ct_out_ref = kept
        for i in range(3):
            y_ref[i] = y[i]
        ct_out_ref[...] = ct
    row = iota((8, 128), 0)
    scal = jnp.where(row == 0, inner_now, jnp.where(row == 1, curve, beta))
    scal_ref[...] = jnp.where(row == 3, taken, scal)
    rows, width = ct.shape
    msg_ref[0:rows, :] = ct.astype(BF16)
    row = iota((TAIL, width), 0)
    tail = jnp.zeros((TAIL, width), F32)
    for at, value in enumerate([slot_ref[0:1, :], slot_ref[1:2, :], *pieces(taken)]):
        tail = jnp.where(row == at, value, tail)
    msg_ref[rows : rows + TAIL, :] = tail.astype(BF16)


def camera_kernel(masks, first, last, *refs):
    parts = len(masks)
    msgs, refs = refs[:parts], refs[parts:]
    scal_ref, z_ref, cz_ref, r_ref, *refs = refs
    if not first:
        d_old_ref, cd_old_ref, sol_old_ref, *refs = refs
    if last:
        sol_hbm, res_hbm, all_ref, t4_ref, sol_ref, split, sol_out, res_out, sems = refs
    else:
        e_ref, m_ref, c_ref, slot_ref, *refs = refs
        msg_ref, res_ref, sol_ref, zn_ref, czn_ref, *refs = refs
        if not first:
            d_ref, cd_ref, *refs = refs
        all_ref, t4_ref, zt_ref, rows_ref, part_ref = refs
    planes = z_ref.shape[1]
    rows_all = all_ref.shape[1] - TAIL
    me = lax.axis_index("pts")
    odd = lax.axis_index("cam") % 2
    for (even_mask, odd_mask), msg in zip(masks, msgs):
        all_ref[me ^ (even_mask + odd * (odd_mask - even_mask))] = msg[...]
    taken, tiles = [], []
    for k in range(parts):
        tail = all_ref[k, rows_all : rows_all + TAIL, :].astype(F32)
        taken.append(tail[2:3, 0:1] + tail[3:4, 0:1] + tail[4:5, 0:1])
        onehot = tile_onehot(tail, 8 * planes, planes)
        tiles.append(
            lax.dot_general(all_ref[k, 0:rows_all, :], onehot, NT, preferred_element_type=F32)
        )
    inner_now, curve, beta = scal_ref[0:1, 0:1], scal_ref[1:2, 0:1], scal_ref[2:3, 0:1]
    step_size = inner_now / (curve - tree_sum(taken))
    from_tiles(tree_sum(tiles), t4_ref)

    def update_last(g, carry):
        rows = pl.ds(pl.multiple_of(g * 8, 8), 8)
        for j in range(9):
            d = z_ref[j, rows, :] + beta * d_old_ref[j, rows, :]
            c_d = cz_ref[j, rows, :] + beta * cd_old_ref[j, rows, :]
            sol_ref[j, rows, :] = sol_old_ref[j, rows, :] + step_size * d
            t4_ref[j, rows, :] = r_ref[j, rows, :] - step_size * (c_d - t4_ref[j, rows, :])
        return carry

    def write(n, src, wide, dst):
        buffer = split.at[n]
        for j in range(8):
            buffer[pl.ds(j, planes, 8), :] = src[j]
        for a in range(planes):
            wide[0:8, 128 * a : 128 * a + 128] = buffer[8 * a : 8 * a + 8, :]
            wide[8:9, 128 * a : 128 * a + 128] = src[8, a : a + 1, :]
        copy = pltpu.make_async_copy(wide, dst, sems.at[n])
        copy.start()
        return copy

    if last:
        lax.fori_loop(0, planes // 8, update_last, 0, unroll=True)
        copies = [write(0, sol_ref, sol_out, sol_hbm), write(1, t4_ref, res_out, res_hbm)]
        for copy in copies:
            copy.wait()
        return

    def rows_of(g):
        return pl.ds(8 * g, 8)

    direction_of_c = cz_ref if first else cd_ref
    for g in range(planes // 8):
        rows, r = rows_of(g), []
        for j in range(9):
            c_d = cz_ref[j, rows, :]
            if not first:
                c_d = c_d + beta * cd_old_ref[j, rows, :]
                cd_ref[j, rows, :] = c_d
            r.append(r_ref[j, rows, :] - step_size * (c_d - t4_ref[j, rows, :]))
        z = sym_rows(m_ref, 9, rows, r)
        for j in range(9):
            res_ref[j, rows, :] = r[j]
            zn_ref[j, rows, :] = z[j]

    def update(g, sums):
        rows = rows_of(g)
        z = [zn_ref[j, rows, :] for j in range(9)]
        r = [res_ref[j, rows, :] for j in range(9)]
        cd = [direction_of_c[j, rows, :] for j in range(9)]
        cz = sym_rows(c_ref, 9, rows, z)
        for j in range(9):
            czn_ref[j, rows, :] = cz[j]
            d = z_ref[j, rows, :]
            if not first:
                d = d + beta * d_old_ref[j, rows, :]
                d_ref[j, rows, :] = d
            step = step_size * d
            sol_ref[j, rows, :] = step if first else sol_old_ref[j, rows, :] + step
        pairs = (zip(r, z), zip(z, cz), zip(z, cd))
        return [s + tree_sum([a * b for a, b in p]) for s, p in zip(sums, pairs)]

    to_tiles(zn_ref, zt_ref)
    gather_rows(zt_ref, tile_onehot(slot_ref[...], 8 * planes, planes), rows_ref)
    count = e_ref.shape[0]
    sums = [jnp.zeros((8, 128), F32)] * 3
    steps = planes // 8
    for g in range(2 * steps):
        pairs = range(g * count // (4 * steps), (g + 1) * count // (4 * steps))
        forward_pairs(e_ref, rows_ref, part_ref, pairs)
        if g < steps:
            sums = update(g, sums)
    scalars = scalar_lanes([total(s) for s in sums], count)
    msg_ref[...] = jnp.concatenate([forward_sum(part_ref, count), scalars], axis=1).astype(BF16)


def per_device(n_cam, n_pts, rhs, cam_block, coupling, point_inverse, precond, tile_index, tile_count):
    count, slots = tile_index.shape
    size, cams = rhs.shape
    rows, cols = coupling.shape[1:]
    planes, tiles, width = cams // 128, cams // 16, count * slots
    points = point_inverse.shape[2]
    shape = jax.ShapeDtypeStruct
    vector = shape((size, planes, 128), F32)
    message = shape((count, 256), BF16)
    planes_of = size * (size + 1) // 2
    part_scratch = pltpu.VMEM((cols // 128, width, 128), F32)
    rows_scratch = pltpu.VMEM((width, rows), F32)
    cols_scratch = pltpu.VMEM((rows, width), F32)
    zt_scratch = pltpu.VMEM((rows, tiles), BF16)

    def call(kernel, outs, args, in_specs=None, scratch=(), megabytes=8, out_spec=VMEM, name=None):
        return pl.pallas_call(
            kernel,
            out_shape=outs,
            in_specs=in_specs or [VMEM] * len(args),
            out_specs=jax.tree.map(lambda _: out_spec, outs),
            scratch_shapes=list(scratch),
            compiler_params=pltpu.CompilerParams(vmem_limit_bytes=megabytes * 2**20),
            name=name,
        )(*args)

    def exchange(value, axis, axis_size, masks):
        return [value] + [
            lax.ppermute(value, axis, [(i, i ^ k) for i in range(axis_size)]) for k in masks
        ]

    odd_order = (*range(1, n_pts, 2), *range(2, n_pts, 2))
    pts_masks = tuple(zip(odd_order[-1:] + odd_order[:-1], odd_order))

    def points_permute(value, masks):
        pairs = [
            (cam * n_pts + pts, cam * n_pts + (pts ^ masks[cam % 2]))
            for cam in range(n_cam)
            for pts in range(n_pts)
        ]
        return lax.ppermute(value, ("cam", "pts"), pairs)

    coupling, m4, c4, v6, residual, z, cz, slot, message_now = call(
        start_kernel,
        [
            pltpu.VMEM(coupling.shape, BF16),
            pltpu.VMEM((planes_of, planes, 128), F32),
            pltpu.VMEM((planes_of, planes, 128), F32),
            pltpu.VMEM((6, count, 128), F32),
            vector,
            vector,
            vector,
            shape((8, width), F32),
            message,
        ],
        [
            in_hbm(value)
            for value in (
                rhs, precond, cam_block, coupling, point_inverse, tile_index.T, tile_count.T,
            )
        ],
        in_specs=[HBM] * 7,
        scratch=[
            pltpu.VMEM((size, cams), F32),
            pltpu.VMEM((8, 8, cams), F32),
            pltpu.VMEM((size, cams), F32),
            pltpu.VMEM((8, 8, cams), F32),
            pltpu.VMEM((size, cams), F32),
            pltpu.VMEM((3, 3, points), F32),
            pltpu.VMEM((slots, count), jnp.int32),
            pltpu.VMEM((1, count), jnp.int32),
            pltpu.VMEM((2, 8 * planes, 128), F32),
            pltpu.VMEM((points // 128, 128), F32),
            zt_scratch,
            rows_scratch,
            part_scratch,
            pltpu.SemaphoreType.DMA((8,)),
            pltpu.SemaphoreType.DMA((len(FETCHES) - 1,)),
        ],
        megabytes=16,
        name="start",
    )
    inner = max(1, n_cam // 4)
    old_points, old_camera = (), ()
    for iteration in range(ITERS):
        first, last = iteration == 0, iteration + 1 == ITERS
        if inner > 1:
            pair = exchange(message_now, "cam", n_cam, range(1, inner))
            message_now = call(pair_kernel, message, pair, name="pair")
        parts = exchange(message_now, "cam", n_cam, range(inner, n_cam, inner))
        outs = [shape((rows + TAIL, width), BF16), shape((8, 128), F32)]
        kept = [] if last else [shape((3, count, 64), F32), shape((rows, width), F32)]
        tile_message, scal, *kept = call(
            functools.partial(points_kernel, len(parts), first, last),
            outs + kept,
            (*parts, *old_points, coupling, v6, slot),
            scratch=[pltpu.VMEM((count, cols), F32), rows_scratch, cols_scratch],
            name="points",
        )
        old_points = (scal, *kept)
        parts = [tile_message] + [points_permute(tile_message, masks) for masks in pts_masks]
        kernel = functools.partial(camera_kernel, ((0, 0), *pts_masks), first, last)
        common = [
            pltpu.VMEM((n_pts, rows + TAIL, width), BF16),
            pltpu.VMEM((size, planes, 128), F32),
        ]
        args = (*parts, scal, z, cz, residual, *old_camera)
        if last:
            plain = shape((size, cams), F32)
            scratch = [
                *common,
                pltpu.VMEM((size, planes, 128), F32),
                pltpu.VMEM((2, 8 * planes, 128), F32),
                pltpu.VMEM((size, cams), F32),
                pltpu.VMEM((size, cams), F32),
                pltpu.SemaphoreType.DMA((2,)),
            ]
            return tuple(
                call(kernel, [plain, plain], args, scratch=scratch, out_spec=HBM, name="finish")
            )
        outs = [message, vector, vector, vector, vector] + ([] if first else [vector, vector])
        message_now, residual, solution, z_new, cz_new, *direction = call(
            kernel,
            outs,
            (*args, coupling, m4, c4, slot),
            scratch=[*common, zt_scratch, rows_scratch, part_scratch],
            name="camera",
        )
        d, cd = direction if direction else (z, cz)
        old_camera = (d, cd, solution)
        z, cz = z_new, cz_new


def solution(mesh):
    in_specs = (
        P(None, "cam"),
        P(None, None, "cam"),
        P("pts", None, "cam"),
        P(None, None, "pts"),
        P(None, None, "cam"),
        P("pts", "cam"),
        P("pts", "cam"),
    )
    out_specs = (P(None, "cam"), P(None, "cam"))
    return jax.shard_map(
        functools.partial(per_device, mesh.shape["cam"], mesh.shape["pts"]),
        mesh=mesh,
        in_specs=in_specs,
        out_specs=out_specs,
        check_vma=False,
    )
```

```python
import functools

import jax
import jax.numpy as jnp
from jax import lax
from jax.experimental import pallas as pl
from jax.experimental.pallas import tpu as pltpu
from jax.sharding import PartitionSpec as P


ITERS = 3
F32 = jnp.float32
BF16 = jnp.bfloat16
VMEM = pl.BlockSpec(memory_space=pltpu.VMEM)
HBM = pl.BlockSpec(memory_space=pltpu.HBM)
NT = (((1,), (1,)), ((), ()))
FETCHES = (0, 16, 40, 56, 64)
TAIL = 8
BACKWARD_SHARE = 6


def in_hbm(value):
    return pltpu.with_memory_space_constraint(value, pltpu.HBM)


def iota(shape, dim):
    return lax.broadcasted_iota(jnp.int32, shape, dim)


def tree_sum(values):
    while len(values) > 1:
        values = [a + b for a, b in zip(values[::2], values[1::2])] + values[
            len(values) - len(values) % 2 :
        ]
    return values[0]


def sym(size, i, j):
    i, j = min(i, j), max(i, j)
    return i * size - i * (i - 1) // 2 + (j - i)


def total(value):
    return jnp.sum(value, keepdims=True)


def pieces(value):
    high = value.astype(BF16).astype(F32)
    rest = value - high
    middle = rest.astype(BF16).astype(F32)
    return [high, middle, rest - middle]


def scalar_lanes(scalars, rows):
    lane = iota((rows, 64), 1)
    tile = jnp.zeros((rows, 64), F32)
    for at, piece in enumerate(p for s in scalars for p in pieces(s)):
        tile = jnp.where(lane == at, piece, tile)
    return tile


def read_scalars(tile, count):
    row = tile[0:1, :]
    number = iota(row.shape, 1) % 16 // 3
    return [total(jnp.where(number == n, row, 0.0)) for n in range(count)]


def sym_rows(matrix, size, rows, vector):
    return [
        tree_sum([matrix[sym(size, i, j), rows, :] * vector[j] for j in range(size)])
        for i in range(size)
    ]


def tile_onehot(rows, tiles, planes):
    row_a, row_q = rows[0:1, :], rows[1:2, :]
    at = jnp.where(row_a >= 0, row_q * planes + row_a, -1.0).astype(jnp.int32)
    return jnp.where(iota((tiles, at.shape[1]), 0) == at, 1.0, 0.0).astype(BF16)


def swap_halves(even, odd):
    low = iota(even.shape, 1) < 64
    return (
        jnp.where(low, even, pltpu.roll(odd, 64, 1)),
        jnp.where(low, pltpu.roll(even, 64, 1), odd),
    )


def plane_pairs(size):
    return [(j, min(j + 1, size - 1)) for j in range(0, size, 2)]


def to_tiles(z_ref, zt_ref):
    for pair in plane_pairs(z_ref.shape[0]):
        turned = jnp.concatenate([z_ref[j] for j in pair], axis=0).T
        for h in range(4):
            even, odd = (turned[16 * q : 16 * q + 16, :] for q in (2 * h, 2 * h + 1))
            for j, block in zip(pair, swap_halves(even, odd)):
                zt_ref[16 * j : 16 * j + 16, 128 * h : 128 * h + 128] = block.astype(BF16)


def from_tiles(tiles, t4_ref):
    planes = t4_ref.shape[1]
    for pair in plane_pairs(t4_ref.shape[0]):
        blocks = []
        for h in range(4):
            first, second = (
                tiles[16 * j : 16 * j + 16, 128 * h : 128 * h + 128] for j in pair
            )
            blocks += swap_halves(first, second)
        turned = jnp.concatenate(blocks, axis=0).T
        for n, j in enumerate(pair):
            t4_ref[j] = turned[n * planes : (n + 1) * planes, :]


def gather_rows(zt_ref, onehot, rows_ref):
    rows_ref[...] = jnp.dot(zt_ref[...], onehot, preferred_element_type=F32).T


def on_vector_unit(pair, share):
    return (pair + 1) * share // 16 > pair * share // 16


def forward_pairs(e_ref, rows_ref, part_ref, pairs):
    sub = iota((8, rows_ref.shape[1]), 0)
    for pair in pairs:
        at = pl.ds(8 * pair, 8)
        both = rows_ref[at, :]
        top = jnp.where(sub < 4, both, 0.0).astype(BF16)
        low = jnp.where(sub >= 4, both, 0.0).astype(BF16)
        part = jnp.dot(top, e_ref[2 * pair], preferred_element_type=F32) + jnp.dot(
            low, e_ref[2 * pair + 1], preferred_element_type=F32
        )
        for i in range(part_ref.shape[0]):
            part_ref[i, at, :] = part[:, 128 * i : 128 * i + 128]


def forward_sum(part_ref, count):
    def pick(i, s):
        return part_ref[i, pl.ds(s, count, 4), :]

    even = jnp.concatenate([pick(0, 0) + pick(3, 2), pick(1, 0) + pick(4, 2)], axis=1)
    odd = jnp.concatenate([pick(1, 1) + pick(4, 3), pick(2, 1) + pick(5, 3)], axis=1)
    return even[:, :192] + odd[:, 64:]


def backward(e_ref, y, yc_ref, rows_ref, cols_ref):
    count, rows = e_ref.shape[:2]
    wide = [jnp.concatenate(pair, axis=1) for pair in ((y[0], y[1]), (y[2], y[0]), (y[1], y[2]))]
    for i in range(6):
        yc_ref[:, 128 * i : 128 * i + 128] = wide[i % 3]
    row, col = iota((8, 768), 0), iota((8, 768), 1)
    masks = [(col >= 192 * (row - r)) & (col < 192 * (row - r) + 192) for r in (0, 4)]
    low_lanes = iota((1, 128), 1) < 64
    for pair in range(count // 2):
        if on_vector_unit(pair, BACKWARD_SHARE):
            for t in (2 * pair, 2 * pair + 1):
                e = [e_ref[t, :, 128 * i : 128 * i + 128].astype(F32) for i in range(6)]
                w = [yc_ref[pl.ds(t, 1), 128 * i : 128 * i + 128] for i in range(3)]
                w_low, w_high = jnp.where(low_lanes, w[1], 0.0), jnp.where(low_lanes, 0.0, w[1])
                sums = (
                    e[0] * w[0] + e[1] * w_low,
                    e[1] * w_high + e[2] * w[2],
                    e[3] * w[0] + e[4] * w_low,
                    e[4] * w_high + e[5] * w[2],
                )
                for s, value in enumerate(sums):
                    cols_ref[:, 4 * t + s : 4 * t + s + 1] = jnp.sum(value, axis=1, keepdims=True)
            continue
        part = None
        for k in range(2):
            wide_row = jnp.broadcast_to(yc_ref[pl.ds(2 * pair + k, 1), :], (8, 768))
            lhs = jnp.where(masks[k], wide_row, 0.0).astype(BF16)
            one = lax.dot_general(lhs, e_ref[2 * pair + k], NT, preferred_element_type=F32)
            part = one if part is None else part + one
        rows_ref[pl.ds(8 * pair, 8), :] = part
    pair_of = iota((rows, 4 * count), 1) // 8
    vector = on_vector_unit(pair_of, BACKWARD_SHARE)
    return jnp.where(vector, cols_ref[...], rows_ref[...].T)


def start_kernel(
    rhs_hbm, m_hbm, c_hbm, e_hbm, v_hbm, index_hbm, count_hbm,
    e_ref, m_ref, c_ref, v_ref, r_ref, z_ref, cz_ref, slot_ref, msg_ref,
    rn, mn, m8, cn, c8, vn, index_ref, count_ref, split, vrow, zt_ref, rows_ref, part_ref, sems, e_sems,
):
    planes, count = r_ref.shape[1], e_ref.shape[0]
    ends = [count * end // 64 for end in FETCHES]
    parts = list(zip(ends[:-1], ends[1:]))
    inner = pl.ds(0, 8)

    def fetch(n):
        part = pl.ds(parts[n][0], parts[n][1] - parts[n][0])
        return pltpu.make_async_copy(e_hbm.at[part], e_ref.at[part], e_sems.at[n])

    def copy(n, src, dst):
        return pltpu.make_async_copy(src, dst, sems.at[n])

    indices = [copy(0, index_hbm, index_ref), copy(1, count_hbm, count_ref)]
    rhs = [copy(2, rhs_hbm, rn)]
    precond = [copy(3, m_hbm.at[inner, inner], mn), copy(4, m_hbm.at[8], m8)]
    camera = [copy(5, c_hbm.at[inner, inner], cn), copy(6, c_hbm.at[8], c8)]
    inverse = [copy(7, v_hbm, vn)]
    early = [fetch(n) for n in range(2)]
    late = [fetch(n) for n in range(2, len(parts))]
    for one in rhs + precond + indices + early + camera + inverse + late:
        one.start()

    def wait(copies):
        for one in copies:
            one.wait()

    def split_rows(src, buffer, used):
        for a in range(src.shape[1] // 128):
            buffer[8 * a : 8 * a + used, :] = src[0:used, 128 * a : 128 * a + 128]

    def split_last(src, out_ref, at):
        for a in range(planes):
            out_ref[at, a : a + 1, :] = src[8:9, 128 * a : 128 * a + 128]

    def split_matrix(inner_ref, last_ref, out_ref):
        for i in range(9):
            buffer = split.at[i % 2]
            split_rows(inner_ref.at[i] if i < 8 else last_ref, buffer, 8)
            for j in range(i if i < 8 else 0, 8):
                out_ref[sym(9, i, j)] = buffer[pl.ds(j, planes, 8), :]
        split_last(last_ref, out_ref, sym(9, 8, 8))

    wait(rhs)
    split_rows(rn, split.at[0], 8)
    for j in range(8):
        r_ref[j] = split[0, pl.ds(j, planes, 8), :]
    split_last(rn, r_ref, 8)

    wait(indices)
    slots = index_ref.shape[0]
    width = count * slots
    index = index_ref[...]
    used = iota(index.shape, 0) < count_ref[...]
    spread = jnp.where(iota((count, width), 1) // slots == iota((count, width), 0), 1.0, 0.0)
    mine = iota((8, width), 1) % slots == iota((8, width), 0)
    pad = jnp.zeros((8 - slots, count), F32)
    slot_rows = []
    for part in (jnp.where(used, index // 8, -1), index % 8):
        padded = jnp.concatenate([part.astype(F32), pad], axis=0).astype(BF16)
        moved = jnp.dot(padded, spread.astype(BF16), preferred_element_type=F32)
        slot_rows.append(jnp.sum(jnp.where(mine, moved, 0.0), axis=0, keepdims=True))
    row = iota((8, width), 0)
    slot_ref[...] = jnp.where(row == 0, slot_rows[0], jnp.where(row == 1, slot_rows[1], 0.0))
    onehot = tile_onehot(slot_ref[...], 8 * planes, planes)

    wait(precond)
    split_matrix(mn, m8, m_ref)

    def precondition(g, inner_sum):
        rows = pl.ds(pl.multiple_of(g * 8, 8), 8)
        r = [r_ref[j, rows, :] for j in range(9)]
        z = sym_rows(m_ref, 9, rows, r)
        for j in range(9):
            z_ref[j, rows, :] = z[j]
        return inner_sum + tree_sum([a * b for a, b in zip(r, z)])

    zero = jnp.zeros((8, 128), F32)
    inner_sum = lax.fori_loop(0, planes // 8, precondition, zero, unroll=True)
    to_tiles(z_ref, zt_ref)
    gather_rows(zt_ref, onehot, rows_ref)

    def forward_chunk(n, one):
        one.wait()
        forward_pairs(e_ref, rows_ref, part_ref, range(parts[n][0] // 2, parts[n][1] // 2))

    for n, one in enumerate(early):
        forward_chunk(n, one)

    wait(camera)
    split_matrix(cn, c8, c_ref)

    def apply_camera(g, curve):
        rows = pl.ds(pl.multiple_of(g * 8, 8), 8)
        z = [z_ref[j, rows, :] for j in range(9)]
        cz = sym_rows(c_ref, 9, rows, z)
        for j in range(9):
            cz_ref[j, rows, :] = cz[j]
        return curve + tree_sum([a * b for a, b in zip(z, cz)])

    curve = lax.fori_loop(0, planes // 8, apply_camera, zero, unroll=True)

    wait(inverse)
    half = vrow.shape[0]
    for i in range(3):
        split_rows(vn.at[i], split.at[i % 2], 3)
        for j in range(i, 3):
            plane = split[i % 2, pl.ds(j, half, 8), :]
            v_ref[sym(3, i, j), pl.ds(0, half, 2), :] = plane
            v_ref[sym(3, i, j), pl.ds(1, half, 2), :] = jnp.concatenate(
                [plane[:, 64:], plane[:, :64]], axis=1
            )

    for n, one in enumerate(late):
        forward_chunk(len(early) + n, one)
    scalars = scalar_lanes([total(inner_sum), total(curve), jnp.zeros((1, 1), F32)], count)
    msg_ref[...] = jnp.concatenate([forward_sum(part_ref, count), scalars], axis=1).astype(BF16)


def pair_kernel(*refs):
    *in_refs, out_ref = refs
    values = [ref[...].astype(F32) for ref in in_refs]
    scalars = []
    for k, value in enumerate(values):
        lanes = value[:, 192:]
        if k > 0:
            lanes = jnp.concatenate([lanes[:, 64 - 16 * k :], lanes[:, : 64 - 16 * k]], axis=1)
        scalars.append(lanes)
    points = tree_sum([value[:, :192] for value in values])
    out_ref[...] = jnp.concatenate([points, tree_sum(scalars)], axis=1).astype(BF16)


def points_kernel(parts, first, last, *refs):
    summed = tree_sum([ref[...].astype(F32) for ref in refs[:parts]])
    refs = refs[parts:]
    if not first:
        scal_old_ref, y_old_ref, ct_old_ref, *refs = refs
    e_ref, v_ref, slot_ref, msg_ref, scal_ref, *refs = refs
    *kept, yc_ref, c_ref, ct_ref = refs
    inner_now, z_c_z, z_c_d = read_scalars(summed[:, 192:], 3)
    beta, curve = jnp.zeros((1, 1), F32), z_c_z
    if not first:
        beta = inner_now / scal_old_ref[0:1, 0:1]
        curve = z_c_z + beta * (2.0 * z_c_d + beta * scal_old_ref[1:2, 0:1])
    p = [summed[:, 64 * i : 64 * i + 64] for i in range(3)]
    y = [tree_sum([v_ref[sym(3, i, j)][:, :64] * p[j] for j in range(3)]) for i in range(3)]
    taken = total(tree_sum([a * b for a, b in zip(p, y)]))
    ct = backward(e_ref, y, yc_ref, c_ref, ct_ref)
    if not first:
        crossed = total(tree_sum([p[i] * y_old_ref[i] for i in range(3)]))
        taken = taken + beta * (2.0 * crossed + beta * scal_old_ref[3:4, 0:1])
        ct = ct + beta * ct_old_ref[...]
        y = [y[i] + beta * y_old_ref[i] for i in range(3)]
    if not last:
        y_ref, ct_out_ref = kept
        for i in range(3):
            y_ref[i] = y[i]
        ct_out_ref[...] = ct
    row = iota((8, 128), 0)
    scal = jnp.where(row == 0, inner_now, jnp.where(row == 1, curve, beta))
    scal_ref[...] = jnp.where(row == 3, taken, scal)
    rows, width = ct.shape
    msg_ref[0:rows, :] = ct.astype(BF16)
    row = iota((TAIL, width), 0)
    tail = jnp.zeros((TAIL, width), F32)
    for at, value in enumerate([slot_ref[0:1, :], slot_ref[1:2, :], *pieces(taken)]):
        tail = jnp.where(row == at, value, tail)
    msg_ref[rows : rows + TAIL, :] = tail.astype(BF16)


def camera_kernel(masks, first, last, *refs):
    parts = len(masks)
    msgs, refs = refs[:parts], refs[parts:]
    scal_ref, z_ref, cz_ref, r_ref, *refs = refs
    if not first:
        d_old_ref, cd_old_ref, sol_old_ref, *refs = refs
    if last:
        sol_hbm, res_hbm, all_ref, t4_ref, sol_ref, split, sol_out, res_out, sems = refs
    else:
        e_ref, m_ref, c_ref, slot_ref, *refs = refs
        msg_ref, res_ref, sol_ref, zn_ref, czn_ref, *refs = refs
        if not first:
            d_ref, cd_ref, *refs = refs
        all_ref, t4_ref, zt_ref, rows_ref, part_ref = refs
    planes = z_ref.shape[1]
    rows_all = all_ref.shape[1] - TAIL
    me = lax.axis_index("pts")
    odd = lax.axis_index("cam") % 2
    for (even_mask, odd_mask), msg in zip(masks, msgs):
        all_ref[me ^ (even_mask + odd * (odd_mask - even_mask))] = msg[...]
    tails = [all_ref[k, rows_all : rows_all + TAIL, :].astype(F32) for k in range(parts)]
    taken = [tail[2:3, 0:1] + tail[3:4, 0:1] + tail[4:5, 0:1] for tail in tails]
    inner_now, curve, beta = scal_ref[0:1, 0:1], scal_ref[1:2, 0:1], scal_ref[2:3, 0:1]
    step_size = inner_now / (curve - tree_sum(taken))

    def write(n, src, wide, dst):
        buffer = split.at[n]
        for j in range(8):
            buffer[pl.ds(j, planes, 8), :] = src[j]
        for a in range(planes):
            wide[0:8, 128 * a : 128 * a + 128] = buffer[8 * a : 8 * a + 8, :]
            wide[8:9, 128 * a : 128 * a + 128] = src[8, a : a + 1, :]
        copy = pltpu.make_async_copy(wide, dst, sems.at[n])
        copy.start()
        return copy

    def rows_of(g):
        return pl.ds(8 * g, 8)

    copies = []
    if last:
        for g in range(planes // 8):
            rows = rows_of(g)
            for j in range(9):
                d = z_ref[j, rows, :] + beta * d_old_ref[j, rows, :]
                sol_ref[j, rows, :] = sol_old_ref[j, rows, :] + step_size * d
        copies.append(write(0, sol_ref, sol_out, sol_hbm))
    tiles = []
    for k in range(parts):
        onehot = tile_onehot(tails[k], 8 * planes, planes)
        tiles.append(
            lax.dot_general(all_ref[k, 0:rows_all, :], onehot, NT, preferred_element_type=F32)
        )
    from_tiles(tree_sum(tiles), t4_ref)
    if last:
        for g in range(planes // 8):
            rows = rows_of(g)
            for j in range(9):
                c_d = cz_ref[j, rows, :] + beta * cd_old_ref[j, rows, :]
                t4_ref[j, rows, :] = r_ref[j, rows, :] - step_size * (c_d - t4_ref[j, rows, :])
        copies.append(write(1, t4_ref, res_out, res_hbm))
        for copy in copies:
            copy.wait()
        return

    direction_of_c = cz_ref if first else cd_ref
    for g in range(planes // 8):
        rows, r = rows_of(g), []
        for j in range(9):
            c_d = cz_ref[j, rows, :]
            if not first:
                c_d = c_d + beta * cd_old_ref[j, rows, :]
                cd_ref[j, rows, :] = c_d
            r.append(r_ref[j, rows, :] - step_size * (c_d - t4_ref[j, rows, :]))
        z = sym_rows(m_ref, 9, rows, r)
        for j in range(9):
            res_ref[j, rows, :] = r[j]
            zn_ref[j, rows, :] = z[j]

    def update(g, sums):
        rows = rows_of(g)
        z = [zn_ref[j, rows, :] for j in range(9)]
        r = [res_ref[j, rows, :] for j in range(9)]
        cd = [direction_of_c[j, rows, :] for j in range(9)]
        cz = sym_rows(c_ref, 9, rows, z)
        for j in range(9):
            czn_ref[j, rows, :] = cz[j]
            d = z_ref[j, rows, :]
            if not first:
                d = d + beta * d_old_ref[j, rows, :]
                d_ref[j, rows, :] = d
            step = step_size * d
            sol_ref[j, rows, :] = step if first else sol_old_ref[j, rows, :] + step
        pairs = (zip(r, z), zip(z, cz), zip(z, cd))
        return [s + tree_sum([a * b for a, b in p]) for s, p in zip(sums, pairs)]

    to_tiles(zn_ref, zt_ref)
    gather_rows(zt_ref, tile_onehot(slot_ref[...], 8 * planes, planes), rows_ref)
    count = e_ref.shape[0]
    sums = [jnp.zeros((8, 128), F32)] * 3
    steps = planes // 8
    for g in range(2 * steps):
        pairs = range(g * count // (4 * steps), (g + 1) * count // (4 * steps))
        forward_pairs(e_ref, rows_ref, part_ref, pairs)
        if g < steps:
            sums = update(g, sums)
    scalars = scalar_lanes([total(s) for s in sums], count)
    msg_ref[...] = jnp.concatenate([forward_sum(part_ref, count), scalars], axis=1).astype(BF16)


def per_device(n_cam, n_pts, rhs, cam_block, coupling, point_inverse, precond, tile_index, tile_count):
    count, slots = tile_index.shape
    size, cams = rhs.shape
    rows, cols = coupling.shape[1:]
    planes, tiles, width = cams // 128, cams // 16, count * slots
    points = point_inverse.shape[2]
    shape = jax.ShapeDtypeStruct
    vector = shape((size, planes, 128), F32)
    message = shape((count, 256), BF16)
    planes_of = size * (size + 1) // 2
    part_scratch = pltpu.VMEM((cols // 128, width, 128), F32)
    rows_scratch = pltpu.VMEM((width, rows), F32)
    cols_scratch = pltpu.VMEM((rows, width), F32)
    zt_scratch = pltpu.VMEM((rows, tiles), BF16)

    def call(kernel, outs, args, in_specs=None, scratch=(), megabytes=8, out_spec=VMEM, name=None):
        return pl.pallas_call(
            kernel,
            out_shape=outs,
            in_specs=in_specs or [VMEM] * len(args),
            out_specs=jax.tree.map(lambda _: out_spec, outs),
            scratch_shapes=list(scratch),
            compiler_params=pltpu.CompilerParams(vmem_limit_bytes=megabytes * 2**20),
            name=name,
        )(*args)

    def exchange(value, axis, axis_size, masks):
        return [value] + [
            lax.ppermute(value, axis, [(i, i ^ k) for i in range(axis_size)]) for k in masks
        ]

    odd_order = (*range(1, n_pts, 2), *range(2, n_pts, 2))
    pts_masks = tuple(zip(odd_order[-1:] + odd_order[:-1], odd_order))

    def points_permute(value, masks):
        pairs = [
            (cam * n_pts + pts, cam * n_pts + (pts ^ masks[cam % 2]))
            for cam in range(n_cam)
            for pts in range(n_pts)
        ]
        return lax.ppermute(value, ("cam", "pts"), pairs)

    coupling, m4, c4, v6, residual, z, cz, slot, message_now = call(
        start_kernel,
        [
            pltpu.VMEM(coupling.shape, BF16),
            pltpu.VMEM((planes_of, planes, 128), F32),
            pltpu.VMEM((planes_of, planes, 128), F32),
            pltpu.VMEM((6, count, 128), F32),
            vector,
            vector,
            vector,
            shape((8, width), F32),
            message,
        ],
        [
            in_hbm(value)
            for value in (
                rhs, precond, cam_block, coupling, point_inverse, tile_index.T, tile_count.T,
            )
        ],
        in_specs=[HBM] * 7,
        scratch=[
            pltpu.VMEM((size, cams), F32),
            pltpu.VMEM((8, 8, cams), F32),
            pltpu.VMEM((size, cams), F32),
            pltpu.VMEM((8, 8, cams), F32),
            pltpu.VMEM((size, cams), F32),
            pltpu.VMEM((3, 3, points), F32),
            pltpu.VMEM((slots, count), jnp.int32),
            pltpu.VMEM((1, count), jnp.int32),
            pltpu.VMEM((2, 8 * planes, 128), F32),
            pltpu.VMEM((points // 128, 128), F32),
            zt_scratch,
            rows_scratch,
            part_scratch,
            pltpu.SemaphoreType.DMA((8,)),
            pltpu.SemaphoreType.DMA((len(FETCHES) - 1,)),
        ],
        megabytes=16,
        name="start",
    )
    inner = max(1, n_cam // 4)
    old_points, old_camera = (), ()
    for iteration in range(ITERS):
        first, last = iteration == 0, iteration + 1 == ITERS
        if inner > 1:
            pair = exchange(message_now, "cam", n_cam, range(1, inner))
            message_now = call(pair_kernel, message, pair, name="pair")
        parts = exchange(message_now, "cam", n_cam, range(inner, n_cam, inner))
        outs = [shape((rows + TAIL, width), BF16), shape((8, 128), F32)]
        kept = [] if last else [shape((3, count, 64), F32), shape((rows, width), F32)]
        tile_message, scal, *kept = call(
            functools.partial(points_kernel, len(parts), first, last),
            outs + kept,
            (*parts, *old_points, coupling, v6, slot),
            scratch=[pltpu.VMEM((count, cols), F32), rows_scratch, cols_scratch],
            name="points",
        )
        old_points = (scal, *kept)
        parts = [tile_message] + [points_permute(tile_message, masks) for masks in pts_masks]
        kernel = functools.partial(camera_kernel, ((0, 0), *pts_masks), first, last)
        common = [
            pltpu.VMEM((n_pts, rows + TAIL, width), BF16),
            pltpu.VMEM((size, planes, 128), F32),
        ]
        args = (*parts, scal, z, cz, residual, *old_camera)
        if last:
            plain = shape((size, cams), F32)
            scratch = [
                *common,
                pltpu.VMEM((size, planes, 128), F32),
                pltpu.VMEM((2, 8 * planes, 128), F32),
                pltpu.VMEM((size, cams), F32),
                pltpu.VMEM((size, cams), F32),
                pltpu.SemaphoreType.DMA((2,)),
            ]
            return tuple(
                call(kernel, [plain, plain], args, scratch=scratch, out_spec=HBM, name="finish")
            )
        outs = [message, vector, vector, vector, vector] + ([] if first else [vector, vector])
        message_now, residual, solution, z_new, cz_new, *direction = call(
            kernel,
            outs,
            (*args, coupling, m4, c4, slot),
            scratch=[*common, zt_scratch, rows_scratch, part_scratch],
            name="camera",
        )
        d, cd = direction if direction else (z, cz)
        old_camera = (d, cd, solution)
        z, cz = z_new, cz_new


def solution(mesh):
    in_specs = (
        P(None, "cam"),
        P(None, None, "cam"),
        P("pts", None, "cam"),
        P(None, None, "pts"),
        P(None, None, "cam"),
        P("pts", "cam"),
        P("pts", "cam"),
    )
    out_specs = (P(None, "cam"), P(None, "cam"))
    return jax.shard_map(
        functools.partial(per_device, mesh.shape["cam"], mesh.shape["pts"]),
        mesh=mesh,
        in_specs=in_specs,
        out_specs=out_specs,
        check_vma=False,
    )
```
